512 devices in a mesh: rep: 32 (over z, x), fsdp: 16 (over y, core).
Axes of the slice: x: 4, y: 8, z: 8, core: 2. Of those that a mesh axis runs over, the one named last changes fastest.
Arguments:
- grad_parts: bfloat16 [32, 16, 256, 6144], P('rep', 'fsdp'), may hold values from -5 to 5
- momentum: float32 [32, 256, 6144], P('rep', None, 'fsdp'), may hold values from -6 to 6
- keep_counts: int32 [32, 4, 96], P('rep', None, 'fsdp'), may hold values from 1 to 16, as said below
- keep_blocks: int32 [32, 4, 96, 16], P('rep', None, 'fsdp'), may hold values from 0 to 63, as said below
Outputs:
- update: float32 [256, 6144], P(None, 'fsdp')
- new_momentum: float32 [32, 256, 6144], P('rep', None, 'fsdp')
The draws below stay inside these ranges and needn't reach their ends.
Inputs may be any that keep to these rules, and one draw needn't show every extreme that they name: `keep_counts`: every replica has a span that keeps exactly 16 blocks. `keep_blocks`: in each span the 16 entries are distinct block numbers; only the first keep_counts of them are kept.
All inputs are finite; a program needn't handle non-finite values.
Results may differ from the reference program's by a relative error of at most 0.0003.
Values sent between devices are 32-bit elements; how exact they have to be, the bound alone decides.
A program may use at most 64 MiB of HBM per device.

```python
import jax
import jax.numpy as jnp
from jax import lax

D = 6144
ROWS = 256
SPAN = 64
GRID = 8
KMAX = 16
N_REP = 32
N_FSDP = 16


def draw_keep_counts(key, part):
    key = jax.random.fold_in(key, 11)
    first_key, second_key, third_key = jax.random.split(key, 3)
    shape = (N_REP, ROWS // SPAN, D // SPAN)
    column_caps = jax.random.randint(first_key, (1, 1, D // SPAN), 2, KMAX + 1)
    counts = 1 + jax.random.randint(second_key, shape, 0, 4096) % column_caps
    heavy = jax.random.randint(third_key, (N_REP, 1, 1), 0, D // SPAN)
    row_ids = jnp.arange(ROWS // SPAN, dtype=jnp.int32)[None, :, None]
    col_ids = jnp.arange(D // SPAN, dtype=jnp.int32)[None, None, :]
    counts = jnp.where((row_ids == 0) & (col_ids == heavy), KMAX, counts)
    return counts.astype(jnp.int32)


def draw_keep_blocks(key, part):
    key = jax.random.fold_in(key, 23)
    shape = (N_REP, ROWS // SPAN, D // SPAN, GRID * GRID)
    scores = jax.random.randint(key, shape, 0, 2 ** 20) * (GRID * GRID) + jnp.arange(GRID * GRID, dtype=jnp.int32)
    order = jnp.argsort(scores, axis=-1, stable=True)
    return order[..., :KMAX].astype(jnp.int32)


def strengthened(array, stream_key, source, target, shards_of, factor):
    owner, partner = [(jnp.arange(array.shape[dim]) // (array.shape[dim] // shards_of)).reshape([-1 if axis == dim else 1 for axis in range(array.ndim)]) for dim in (source, target)]
    chosen = jax.random.permutation(stream_key, shards_of)[partner]
    strong = (owner == chosen) | (owner == (partner + shards_of // 2) % shards_of)
    return jnp.where(strong, factor * array, array)


def block_levels(own_key, shape, shards, least, high):
    def one(axis_at, shards_of):
        heights = jax.random.uniform(jax.random.fold_in(jax.random.fold_in(own_key, 6), axis_at), (shards_of,), jnp.float32, least / len(shards), high / len(shards))
        return jnp.repeat(jnp.exp(heights), shape[axis_at] // shards_of).reshape((-1,) + (1,) * (len(shape) - axis_at - 1))

    level = one(*shards[0])
    for cut in shards[1:]:
        level = level * one(*cut)
    return level


def scatter_about(stream_key, dims, spread, bound, cuts=(), kind=jnp.bfloat16):
    values = spread * jax.random.normal(stream_key, dims, jnp.float32)
    if cuts:
        values = values * block_levels(stream_key, dims, cuts, -0.22, 0.18)
    return jnp.clip(values, -bound, bound).astype(kind)


def bell_draw_with(own_key, shape, width, most, shards, heavy, kind=jnp.bfloat16):
    drawn = width * jax.random.normal(own_key, shape, jnp.float32)
    if shards:
        drawn = drawn * block_levels(own_key, shape, shards, -0.22, 0.18)
    return jnp.clip(strengthened(drawn, jax.random.fold_in(own_key, 3), *heavy), -most, most).astype(kind)


def setup_inputs(seed: int = 0) -> dict:
    splits = jax.random.split(jax.random.key(seed), 5)
    return {
        "grad_parts": bell_draw_with(splits[0], (N_REP, N_FSDP, ROWS, D), 0.25, 5.0, ((0, 32), (1, 16)), (1, 3, 16, 2.0)),
        "momentum": scatter_about(splits[1], (N_REP, ROWS, D), 1.0, 6.0, ((0, 32), (2, 16)), jnp.float32),
        "keep_counts": draw_keep_counts(jax.random.fold_in(splits[4], 71), 0),
        "keep_blocks": draw_keep_blocks(jax.random.fold_in(splits[4], 71), 0),
    }


def dct_table():
    frequency = jnp.arange(SPAN, dtype=jnp.float32)[:, None]
    position = jnp.arange(SPAN, dtype=jnp.float32)[None, :]
    basis = jnp.cos(jnp.pi * (2.0 * position + 1.0) * frequency / (2.0 * SPAN)) * jnp.sqrt(2.0 / SPAN)
    first_scale = jnp.where(frequency == 0.0, jnp.sqrt(0.5), 1.0)
    return basis * first_scale

def keep_mask(counts, block_ids):
    span_rows, span_cols = counts.shape
    slot_ids = jnp.arange(KMAX, dtype=jnp.int32)
    live_slots = slot_ids[None, None, :] < counts[:, :, None]
    numbers = jnp.arange(GRID * GRID, dtype=jnp.int32)
    chosen = jnp.any((block_ids[:, :, :, None] == numbers) & live_slots[:, :, :, None], axis=2)
    chosen = chosen.astype(jnp.float32).reshape(span_rows, span_cols, GRID, GRID)
    block_side = SPAN // GRID
    chosen = jnp.repeat(jnp.repeat(chosen, block_side, axis=2), block_side, axis=3)
    return chosen.transpose(0, 2, 1, 3).reshape(span_rows * SPAN, span_cols * SPAN)

def span_transform(field, left_basis):
    row_count, col_count = field.shape
    spanned = field.reshape(row_count // SPAN, SPAN, col_count // SPAN, SPAN)
    result = jnp.einsum('uk,akbl,vl->aubv', left_basis, spanned, left_basis, precision=lax.Precision.HIGHEST)
    return result.reshape(row_count, col_count)

def reference(grad_parts, momentum, keep_counts, keep_blocks):
    basis = dct_table()

    def per_replica(carry_sum, items):
        grad_slice, moment, counts, block_ids = items
        summed = lax.optimization_barrier(jnp.sum(grad_slice.astype(jnp.float32), axis=0))
        fresh_moment = 0.9 * moment + summed
        coefficients = span_transform(fresh_moment, basis)
        kept_coeff = coefficients * keep_mask(counts, block_ids)
        residual = fresh_moment - span_transform(kept_coeff, basis.T)
        return (carry_sum + kept_coeff, residual)
    start_sum = jnp.zeros((ROWS, D), jnp.float32)
    summed_coeff, new_momentum = lax.scan(per_replica, start_sum, (grad_parts, momentum, keep_counts, keep_blocks))
    update = span_transform(summed_coeff / N_REP, basis.T)
    return (update, new_momentum)
```

```python
import functools

import jax
import jax.numpy as jnp
import numpy as np
from jax import lax
from jax.experimental import pallas as pl
from jax.experimental.pallas import tpu as pltpu
from jax.sharding import PartitionSpec as P

MESH = pl.DeviceIdType.MESH
F32 = jnp.float32
BF16 = jnp.bfloat16

SPAN = 64
GRID = 8
KMAX = 16
NZ, NX, NY, NCORE = 8, 4, 8, 2
ROWS, COLS, WIDE = 256, 384, 6144
CHUNKS = ROWS // SPAN
SPANS = COLS // SPAN
HALF = SPAN // 2
PIECE = SPAN // NZ
STEPS = NY - 1
DISTANCES = (4, 3, -3, 2, -2, 1, -1, 0)
SLOT = {d: i for i, d in enumerate(DISTANCES)}
HIGHEST = lax.Precision.HIGHEST


def dct_tables():
    k = np.arange(SPAN, dtype=np.float64)[:, None]
    n = np.arange(SPAN, dtype=np.float64)[None, :]
    basis = np.cos(np.pi * (2.0 * n + 1.0) * k / (2.0 * SPAN)) * np.sqrt(2.0 / SPAN)
    basis[0] *= np.sqrt(0.5)
    pair = np.kron(np.eye(2), basis)
    spread = (np.arange(COLS)[None, :] // SPAN == np.arange(SPANS)[:, None]).astype(np.float32)
    return (
        basis.astype(np.float32),
        np.ascontiguousarray(basis.T).astype(np.float32),
        pair.astype(np.float32),
        np.ascontiguousarray(pair.T).astype(np.float32),
        spread,
    )


def step_distance(direction, step):
    distance = 4 - (step + 1) // 2
    half = (step + direction) % 2
    return (distance if direction == 0 else -distance), half


def kernel(
    grad, momentum, counts, blocks, c_in, ct_in, pair_in, pairt_in, spread_in,
    update, residual,
    g_v, m_v, cnt_v, blk_v, c_v, ct_v, pair_v, pairt_v, spread_v,
    stage, other, first, ring, mask, res, inv, zbuf, xbuf, upd,
    load_sem, out_sem, pair_send, pair_recv, ring_send, ring_recv,
    z_send, z_recv, x_send, x_recv, a_send, a_recv,
):
    rep, fsdp = lax.axis_index("rep"), lax.axis_index("fsdp")
    z, x = rep // NX, rep % NX
    y, core = fsdp // NCORE, fsdp % NCORE
    peer = {"fsdp": y * NCORE + 1 - core}
    neighbours = (
        {"fsdp": lax.rem(y + 1, NY) * NCORE + core},
        {"fsdp": lax.rem(y + NY - 1, NY) * NCORE + core},
    )

    def at_z(d):
        return {"rep": lax.rem(z + d, NZ) * NX + x}

    def at_x(d):
        return {"rep": z * NX + lax.rem(x + d, NX)}

    partners = (
        [peer, *neighbours]
        + [at_z(d) for d in range(1, NZ)]
        + [at_x(d) for d in range(1, NX)]
    )

    small = [
        (momentum.at[0], m_v), (counts.at[0], cnt_v), (blocks.at[0], blk_v),
        (c_in, c_v), (ct_in, ct_v), (pair_in, pair_v), (pairt_in, pairt_v), (spread_in, spread_v),
    ]
    loads = [
        pltpu.make_async_copy(
            grad.at[0, 0, pl.ds(k * SPAN, SPAN), :],
            g_v.at[pl.ds(k * SPAN, SPAN), :],
            load_sem.at[k],
        )
        for k in range(CHUNKS)
    ] + [
        pltpu.make_async_copy(src, dst, load_sem.at[CHUNKS + i])
        for i, (src, dst) in enumerate(small)
    ]
    for load in loads:
        load.start()

    barrier = pltpu.get_barrier_semaphore()
    for partner in partners:
        pl.semaphore_signal(barrier, inc=1, device_id=partner, device_id_type=MESH)

    def columns(distance, which):
        target = lax.rem(y + distance + NY, NY) * NCORE + which
        return pl.ds(pl.multiple_of(target * COLS, 128), COLS)

    def pair_copy(k, i):
        return pltpu.make_async_remote_copy(
            src_ref=stage.at[k, i],
            dst_ref=other.at[k, i],
            send_sem=pair_send.at[k, i],
            recv_sem=pair_recv.at[k, i],
            device_id=peer,
            device_id_type=MESH,
        )

    def fill_stage(k, i):
        stage[k, i] = g_v[pl.ds(k * SPAN, SPAN), columns(DISTANCES[i], 1 - core)].astype(F32)

    def own(k, distance, half):
        rows = pl.ds(k * SPAN + half * HALF, HALF)
        return (
            g_v[rows, columns(distance, core)].astype(F32)
            + other[k, SLOT[distance], pl.ds(half * HALF, HALF), :]
        )

    def ring_source(direction, k, step):
        return first.at[direction, k, step] if step < 2 else ring.at[direction, k, step - 2]

    def ring_copy(direction, k, step):
        return pltpu.make_async_remote_copy(
            src_ref=ring_source(direction, k, step),
            dst_ref=ring.at[direction, k, step],
            send_sem=ring_send.at[direction, k, step],
            recv_sem=ring_recv.at[direction, k, step],
            device_id=neighbours[direction],
            device_id_type=MESH,
        )

    def ring_step(k, step):
        needed = {0: (4,), 1: (3, -3), 3: (2, -2), 5: (1, -1)}.get(step, ())
        for distance in needed:
            pair_copy(k, SLOT[distance]).wait_recv()
        for direction in (0, 1):
            distance, half = step_distance(direction, step)
            if distance == -4:
                distance = 4
            if step < 2:
                first[direction, k, step] = own(k, distance, half)
            else:
                ring_copy(direction, k, step - 2).wait_recv()
                ring[direction, k, step - 2] += own(k, distance, half)
            ring_copy(direction, k, step).start()

    def make_mask(k):
        spread = spread_v[...]
        numbers = lax.dot_general(
            blk_v[k].astype(F32), spread, (((0,), (0,)), ((), ())),
            precision=HIGHEST, preferred_element_type=F32,
        )
        live = jnp.dot(
            cnt_v[...].astype(F32), spread, precision=HIGHEST, preferred_element_type=F32
        )[k : k + 1, :]
        slot = lax.broadcasted_iota(jnp.int32, (KMAX, COLS), 0).astype(F32)
        column = lax.broadcasted_iota(jnp.int32, (KMAX, COLS), 1)
        place = numbers - ((column % SPAN) // GRID).astype(F32)
        place = jnp.where(slot + 0.5 < live, place, -100.0)
        for u in range(GRID):
            hit = jnp.where(jnp.abs(place - float(u * GRID)) < 0.5, 1.0, 0.0)
            row = jnp.max(hit, axis=0, keepdims=True)
            mask[pl.ds(k * SPAN + u * GRID, GRID), :] = jnp.broadcast_to(row, (GRID, COLS))

    def right(values, table):
        parts = jnp.concatenate([values[:, g * 128 : (g + 1) * 128] for g in range(3)], axis=0)
        done = jnp.dot(parts, table, precision=HIGHEST, preferred_element_type=F32)
        return jnp.concatenate([done[g * SPAN : (g + 1) * SPAN] for g in range(3)], axis=1)

    def z_copy(k, d):
        return pltpu.make_async_remote_copy(
            src_ref=inv.at[k, lax.rem(z + d, NZ)],
            dst_ref=zbuf.at[k, d - 1],
            send_sem=z_send.at[k, d - 1],
            recv_sem=z_recv.at[k, d - 1],
            device_id=at_z(d),
            device_id_type=MESH,
        )

    def x_copy(k, d):
        return pltpu.make_async_remote_copy(
            src_ref=xbuf.at[k, x],
            dst_ref=xbuf.at[k, x],
            send_sem=x_send.at[k, d - 1],
            recv_sem=x_recv.at[k, d - 1],
            device_id=at_x(d),
            device_id_type=MESH,
        )

    def a_copy(k, d):
        return pltpu.make_async_remote_copy(
            src_ref=upd.at[k, z],
            dst_ref=upd.at[k, z],
            send_sem=a_send.at[k, d - 1],
            recv_sem=a_recv.at[k, d - 1],
            device_id=at_z(d),
            device_id_type=MESH,
        )

    def residual_copy(k):
        rows = pl.ds(k * SPAN, SPAN)
        return pltpu.make_async_copy(res.at[rows, :], residual.at[0, rows, :], out_sem.at[0, k])

    def update_copy(k):
        return pltpu.make_async_copy(upd.at[k], update.at[k], out_sem.at[1, k])

    def finish(k):
        pair_copy(k, SLOT[0]).wait_recv()
        for step in (STEPS - 2, STEPS - 1):
            for direction in (0, 1):
                ring_copy(direction, k, step).wait_recv()
        rows = pl.ds(k * SPAN, SPAN)
        lower = own(k, 0, 0) + ring[0, k, STEPS - 1] + ring[1, k, STEPS - 2]
        upper = own(k, 0, 1) + ring[0, k, STEPS - 2] + ring[1, k, STEPS - 1]
        fresh = 0.9 * m_v[rows, :] + jnp.concatenate([lower, upper], axis=0)
        coeff = right(
            jnp.dot(c_v[...], fresh, precision=HIGHEST, preferred_element_type=F32), pairt_v[...]
        )
        kept = coeff * mask[rows, :]
        decoded = right(
            jnp.dot(ct_v[...], kept, precision=HIGHEST, preferred_element_type=F32), pair_v[...]
        )
        inv[k] = decoded.reshape(NZ, PIECE, COLS)
        for d in range(1, NZ):
            z_copy(k, d).start()
        res[rows, :] = fresh - decoded
        residual_copy(k).start()

    def over_x(k):
        for d in range(1, NZ):
            z_copy(k, d).wait_recv()
        xbuf[k, x] = inv[k, z] + jnp.sum(zbuf[k], axis=0)
        for d in range(1, NX):
            x_copy(k, d).start()

    def gather(k):
        for d in range(1, NX):
            x_copy(k, d).wait_recv()
        upd[k, z] = ((xbuf[k, 0] + xbuf[k, 1]) + (xbuf[k, 2] + xbuf[k, 3])) * (1.0 / (NZ * NX))
        for d in range(1, NZ):
            a_copy(k, d).start()

    def put(k):
        for d in range(1, NZ):
            a_copy(k, d).wait_recv()
        update_copy(k).start()

    loads[0].wait()
    for i in range(NY):
        fill_stage(0, i)
    pl.semaphore_wait(barrier, len(partners))
    for i in range(NY):
        pair_copy(0, i).start()
    for load in loads[1:]:
        load.wait()

    for k in range(CHUNKS + 2):
        here, before, ending, older = k < CHUNKS, 0 < k <= CHUNKS, 1 < k, 2 < k
        for offset in range(7):
            if here and offset % 2 == 0:
                ring_step(k, offset // 2)
            if before and offset % 2 == 1:
                ring_step(k - 1, (offset + 7) // 2)
            if k + 1 < CHUNKS:
                for i in (offset,) if offset < 6 else (6, 7):
                    fill_stage(k + 1, i)
                    pair_copy(k + 1, i).start()
            if here and offset == 1:
                make_mask(k)
            last = k == CHUNKS
            if last and offset == 6:
                finish(k - 1)
            if 1 < k <= CHUNKS:
                if offset == 0:
                    finish(k - 2)
                if offset == 3:
                    over_x(k - 2)
                if offset == 5:
                    gather(k - 2)
            if 2 < k <= CHUNKS + 1 and offset == 1:
                put(k - 3)
    k = CHUNKS - 1
    over_x(k)
    gather(k)
    put(k)

    for k in range(CHUNKS):
        residual_copy(k).wait()
        update_copy(k).wait()
        for i in range(NY):
            pair_copy(k, i).wait_send()
        for direction in (0, 1):
            for step in range(STEPS):
                ring_copy(direction, k, step).wait_send()
        for d in range(1, NZ):
            z_copy(k, d).wait_send()
            a_copy(k, d).wait_send()
        for d in range(1, NX):
            x_copy(k, d).wait_send()


def shards(grad_parts, momentum, keep_counts, keep_blocks):
    tables = [jnp.asarray(t) for t in dct_tables()]
    anywhere = pl.BlockSpec(memory_space=pl.ANY)
    dma = pltpu.SemaphoreType.DMA
    update, residual = pl.pallas_call(
        kernel,
        out_shape=(
            jax.ShapeDtypeStruct((CHUNKS, NZ, PIECE, COLS), F32),
            jax.ShapeDtypeStruct((1, ROWS, COLS), F32),
        ),
        in_specs=[anywhere] * 9,
        out_specs=(anywhere, anywhere),
        scratch_shapes=[
            pltpu.VMEM((ROWS, WIDE), BF16),
            pltpu.VMEM((ROWS, COLS), F32),
            pltpu.VMEM((CHUNKS, SPANS), jnp.int32),
            pltpu.VMEM((CHUNKS, SPANS, KMAX), jnp.int32),
            pltpu.VMEM((SPAN, SPAN), F32),
            pltpu.VMEM((SPAN, SPAN), F32),
            pltpu.VMEM((2 * SPAN, 2 * SPAN), F32),
            pltpu.VMEM((2 * SPAN, 2 * SPAN), F32),
            pltpu.VMEM((SPANS, COLS), F32),
            pltpu.VMEM((CHUNKS, NY, SPAN, COLS), F32),
            pltpu.VMEM((CHUNKS, NY, SPAN, COLS), F32),
            pltpu.VMEM((2, CHUNKS, 2, HALF, COLS), F32),
            pltpu.VMEM((2, CHUNKS, STEPS, HALF, COLS), F32),
            pltpu.VMEM((ROWS, COLS), F32),
            pltpu.VMEM((ROWS, COLS), F32),
            pltpu.VMEM((CHUNKS, NZ, PIECE, COLS), F32),
            pltpu.VMEM((CHUNKS, NZ - 1, PIECE, COLS), F32),
            pltpu.VMEM((CHUNKS, NX, PIECE, COLS), F32),
            pltpu.VMEM((CHUNKS, NZ, PIECE, COLS), F32),
            dma((CHUNKS + 8,)),
            dma((2, CHUNKS)),
            dma((CHUNKS, NY)),
            dma((CHUNKS, NY)),
            dma((2, CHUNKS, STEPS)),
            dma((2, CHUNKS, STEPS)),
            dma((CHUNKS, NZ - 1)),
            dma((CHUNKS, NZ - 1)),
            dma((CHUNKS, NX - 1)),
            dma((CHUNKS, NX - 1)),
            dma((CHUNKS, NZ - 1)),
            dma((CHUNKS, NZ - 1)),
        ],
        compiler_params=pltpu.CompilerParams(
            collective_id=0, has_side_effects=True, vmem_limit_bytes=40 * 1024 * 1024
        ),
        cost_estimate=pl.CostEstimate(
            flops=10**9, bytes_accessed=5 * 10**6, transcendentals=0
        ),
    )(grad_parts, momentum, keep_counts, keep_blocks, *tables)
    return update.reshape(ROWS, COLS), residual


def solution(mesh):
    return jax.shard_map(
        shards,
        mesh=mesh,
        in_specs=(
            P("rep", "fsdp", None, None),
            P("rep", None, "fsdp"),
            P("rep", None, "fsdp"),
            P("rep", None, "fsdp", None),
        ),
        out_specs=(P(None, "fsdp"), P("rep", None, "fsdp")),
        check_vma=False,
    )
```

```python
import functools

import jax
import jax.numpy as jnp
import numpy as np
from jax import lax
from jax.experimental import pallas as pl
from jax.experimental.pallas import tpu as pltpu
from jax.sharding import PartitionSpec as P

MESH = pl.DeviceIdType.MESH
F32 = jnp.float32
BF16 = jnp.bfloat16

SPAN = 64
GRID = 8
KMAX = 16
NZ, NX, NY, NCORE = 8, 4, 8, 2
ROWS, COLS, WIDE = 256, 384, 6144
CHUNKS = ROWS // SPAN
SPANS = COLS // SPAN
HALF = SPAN // 2
PIECE = SPAN // NZ
STEPS = NY - 1
VMEM_LIMIT = 62 * 2**20
DISTANCES = (4, 3, -3, 2, -2, 1, -1, 0)
SLOT = {d: i for i, d in enumerate(DISTANCES)}
HIGHEST = lax.Precision.HIGHEST
VMEM_LIMIT = 62 * 2**20
UNITS = ((0, 0, 3), (1, 0, 3), (2, 0, 3), (3, 0, 2), (3, 2, 3))
ORDER = [
    (int(name[0]), int(name[1]))
    for name in (
        "00 10 01 20 02 11 12 03 04 13 14 05 06 15 16 "
        "30 40 21 22 31 32 41 42 23 24 33 34 43 44 25 26 35 36 45 46"
    ).split()
]
FINISH, OVER_X, GATHER, MASK, EXCHANGE = "finish", "over_x", "gather", "mask", "exchange"
TASKS = {
    0: [(EXCHANGE, 2)],
    2: [(EXCHANGE, 3)],
    5: [(MASK, 0)],
    7: [(MASK, 1)],
    9: [(MASK, 2)],
    11: [(MASK, 3)],
    17: [(FINISH, 0)],
    19: [(FINISH, 1)],
    24: [(OVER_X, 0)],
    26: [(OVER_X, 1)],
    28: [(GATHER, 0)],
    30: [(GATHER, 1)],
}
TAIL = [(task, unit) for task in (FINISH, OVER_X, GATHER) for unit in (2, 3, 4)]


def dct_tables():
    k = np.arange(SPAN, dtype=np.float64)[:, None]
    n = np.arange(SPAN, dtype=np.float64)[None, :]
    basis = np.cos(np.pi * (2.0 * n + 1.0) * k / (2.0 * SPAN)) * np.sqrt(2.0 / SPAN)
    basis[0] *= np.sqrt(0.5)
    pair = np.kron(np.eye(2), basis)
    return np.stack([pair.T, pair]).astype(np.float32)


def split_table(table, axis):
    high = table.astype(BF16)
    low = (table - high.astype(F32)).astype(BF16)
    return jnp.concatenate([high, high, low], axis=axis)


def split(values, axis):
    high = values.astype(BF16)
    low = (values - high.astype(F32)).astype(BF16)
    return jnp.concatenate([high, low, high], axis=axis)


def step_distance(direction, step):
    distance = 4 - (step + 1) // 2
    half = (step + direction) % 2
    return (distance if direction == 0 else -distance), half


def kernel(
    grad, momentum, counts, blocks, tables,
    update, residual,
    g_v, m_v, cnt_v, blk_v, tab_v, left_v, right_v,
    stage, other, first, ring, mask, res, inv, zbuf, xbuf, upd,
    load_sem, res_sem, upd_sem, pair_send, pair_recv, ring_send, ring_recv,
    z_send, z_recv, x_send, x_recv, a_send, a_recv,
):
    rep, fsdp = lax.axis_index("rep"), lax.axis_index("fsdp")
    z, x = rep // NX, rep % NX
    y, core = fsdp // NCORE, fsdp % NCORE
    peer = {"fsdp": y * NCORE + 1 - core}
    neighbours = (
        {"fsdp": lax.rem(y + 1, NY) * NCORE + core},
        {"fsdp": lax.rem(y + NY - 1, NY) * NCORE + core},
    )

    def at_z(d):
        return {"rep": lax.rem(z + d, NZ) * NX + x}

    def at_x(d):
        return {"rep": z * NX + lax.rem(x + d, NX)}

    partners = (
        [peer, *neighbours]
        + [at_z(d) for d in range(1, NZ)]
        + [at_x(d) for d in range(1, NX)]
    )

    small = [
        (counts.at[0], cnt_v), (blocks.at[0], blk_v),
        (tables, tab_v), (momentum.at[0], m_v),
    ]
    loads = [
        pltpu.make_async_copy(
            grad.at[0, 0, pl.ds(k * SPAN, SPAN), :],
            g_v.at[pl.ds(k * SPAN, SPAN), :],
            load_sem.at[k],
        )
        for k in range(CHUNKS)
    ] + [
        pltpu.make_async_copy(src, dst, load_sem.at[CHUNKS + i])
        for i, (src, dst) in enumerate(small)
    ]
    for load in loads:
        load.start()

    barrier = pltpu.get_barrier_semaphore()
    for partner in partners:
        pl.semaphore_signal(barrier, inc=1, device_id=partner, device_id_type=MESH)

    def columns(distance, which, first_lane=0, width=COLS):
        target = lax.rem(y + distance + NY, NY) * NCORE + which
        return pl.ds(pl.multiple_of(target * COLS + first_lane, 128), width)

    def lanes(unit):
        _, low, high = UNITS[unit]
        return pl.ds(low * 128, (high - low) * 128)

    def moved(src, dst, send_sem, recv_sem, device):
        return pltpu.make_async_remote_copy(
            src_ref=src, dst_ref=dst, send_sem=send_sem, recv_sem=recv_sem,
            device_id=device, device_id_type=MESH,
        )

    def pair_copy(k, i):
        return moved(stage.at[k, i], other.at[k, i], pair_send, pair_recv.at[k, i], peer)

    def fill_stage(k, i):
        stage[k, i] = g_v[pl.ds(k * SPAN, SPAN), columns(DISTANCES[i], 1 - core)].astype(F32)

    exchanged = set()

    def need(k, distance):
        if (k, distance) not in exchanged:
            exchanged.add((k, distance))
            pair_copy(k, SLOT[distance]).wait_recv()

    def own(unit, distance, half):
        k, low, high = UNITS[unit]
        need(k, distance)
        return (
            g_v[
                pl.ds(k * SPAN + half * HALF, HALF),
                columns(distance, core, low * 128, (high - low) * 128),
            ].astype(F32)
            + other[k, SLOT[distance], pl.ds(half * HALF, HALF), lanes(unit)]
        )

    def ring_copy(direction, unit, step):
        k, window = UNITS[unit][0], lanes(unit)
        return moved(
            first.at[direction, k, step, :, window]
            if step < 2
            else ring.at[direction, k, step - 2, :, window],
            ring.at[direction, k, step, :, window],
            ring_send.at[direction],
            ring_recv.at[direction, unit, step],
            neighbours[direction],
        )

    def ring_step(unit, step):
        k, window = UNITS[unit][0], lanes(unit)
        for direction in (0, 1):
            distance, half = step_distance(direction, step)
            if distance == -4:
                distance = 4
            if step < 2:
                first[direction, k, step, :, window] = own(unit, distance, half)
            else:
                ring_copy(direction, unit, step - 2).wait_recv()
                ring[direction, k, step - 2, :, window] += own(unit, distance, half)
            ring_copy(direction, unit, step).start()

    def make_mask(k):
        spread = jnp.where(
            lax.broadcasted_iota(jnp.int32, (SPANS, COLS), 1) // SPAN
            == lax.broadcasted_iota(jnp.int32, (SPANS, COLS), 0),
            1.0, 0.0,
        )
        numbers = lax.dot_general(
            blk_v[:, k, :].astype(F32), spread, (((0,), (0,)), ((), ())),
            precision=HIGHEST, preferred_element_type=F32,
        )
        live = jnp.dot(
            cnt_v[...].astype(F32), spread, precision=HIGHEST, preferred_element_type=F32
        )[k : k + 1, :]
        slot = lax.broadcasted_iota(jnp.int32, (KMAX, COLS), 0).astype(F32)
        column = lax.broadcasted_iota(jnp.int32, (KMAX, COLS), 1)
        place = numbers - ((column % SPAN) // GRID).astype(F32)
        place = jnp.where(slot + 0.5 < live, place, -100.0)
        for u in range(GRID):
            hit = jnp.where(jnp.abs(place - float(u * GRID)) < 0.5, 1.0, 0.0)
            row = jnp.max(hit, axis=0, keepdims=True)
            mask[pl.ds(k * SPAN + u * GRID, GRID), :] = jnp.broadcast_to(row, (GRID, COLS))

    def transform(values, way):
        groups = values.shape[1] // 128
        rows = jnp.dot(left_v[way], split(values, 0), preferred_element_type=F32)
        parts = jnp.concatenate([rows[:, g * 128 : (g + 1) * 128] for g in range(groups)], axis=0)
        done = jnp.dot(split(parts, 1), right_v[way], preferred_element_type=F32)
        return jnp.concatenate([done[g * SPAN : (g + 1) * SPAN] for g in range(groups)], axis=1)

    def z_copy(unit, d):
        k, window = UNITS[unit][0], lanes(unit)
        return moved(
            inv.at[k, lax.rem(z + d, NZ), :, window], zbuf.at[k, d - 1, :, window],
            z_send, z_recv.at[unit], at_z(d),
        )

    def x_copy(unit, d):
        k, window = UNITS[unit][0], lanes(unit)
        return moved(
            xbuf.at[k, x, :, window], xbuf.at[k, x, :, window],
            x_send, x_recv.at[unit], at_x(d),
        )

    def a_copy(unit, d):
        k, window = UNITS[unit][0], lanes(unit)
        return moved(
            upd.at[k, :, window], update.at[k, z, :, window],
            a_send, a_recv.at[unit], at_z(d),
        )

    def arrived(ref, sem):
        moved(ref, ref, z_send, sem, peer).wait_recv()

    def sent(ref, sem):
        moved(ref, ref, sem, z_recv.at[0], peer).wait_send()

    def residual_copy(unit):
        rows, window = pl.ds(UNITS[unit][0] * SPAN, SPAN), lanes(unit)
        return pltpu.make_async_copy(res.at[rows, window], residual.at[0, rows, window], res_sem)

    def update_copy(unit):
        k, window = UNITS[unit][0], lanes(unit)
        return pltpu.make_async_copy(upd.at[k, :, window], update.at[k, z, :, window], upd_sem)

    def finish(unit):
        k, window = UNITS[unit][0], lanes(unit)
        need(k, 0)
        for step in (STEPS - 2, STEPS - 1):
            for direction in (0, 1):
                ring_copy(direction, unit, step).wait_recv()
        rows = pl.ds(k * SPAN, SPAN)
        lower = (
            own(unit, 0, 0) + ring[0, k, STEPS - 1, :, window] + ring[1, k, STEPS - 2, :, window]
        )
        upper = (
            own(unit, 0, 1) + ring[0, k, STEPS - 2, :, window] + ring[1, k, STEPS - 1, :, window]
        )
        fresh = 0.9 * m_v[rows, window] + jnp.concatenate([lower, upper], axis=0)
        decoded = transform(transform(fresh, 0) * mask[rows, window], 1)
        inv[k, :, :, window] = decoded.reshape(NZ, PIECE, decoded.shape[1])
        for d in (4, 3, 5, 2, 6, 1, 7):
            z_copy(unit, d).start()
        res[rows, window] = fresh - decoded
        residual_copy(unit).start()

    def over_x(unit):
        k, window = UNITS[unit][0], lanes(unit)
        arrived(zbuf.at[k, :, :, window], z_recv.at[unit])
        xbuf[k, x, :, window] = inv[k, z, :, window] + jnp.sum(zbuf[k, :, :, window], axis=0)
        for d in (2, 1, 3):
            x_copy(unit, d).start()

    def gather(unit):
        k, window = UNITS[unit][0], lanes(unit)
        arrived(xbuf.at[k, pl.ds(0, NX - 1), :, window], x_recv.at[unit])
        total = (xbuf[k, 0, :, window] + xbuf[k, 1, :, window]) + (
            xbuf[k, 2, :, window] + xbuf[k, 3, :, window]
        )
        upd[k, :, window] = total * (1.0 / (NZ * NX))
        for d in (4, 3, 5, 2, 6, 1, 7):
            a_copy(unit, d).start()
        update_copy(unit).start()

    def exchange(k):
        for i in range(NY):
            fill_stage(k, i)
            pair_copy(k, i).start()

    loads[0].wait()
    for i in range(NY):
        fill_stage(0, i)
    pl.semaphore_wait(barrier, len(partners))
    for i in range(NY):
        pair_copy(0, i).start()
    for load in loads[1:]:
        load.wait()
    exchange(1)

    tasks = {FINISH: finish, OVER_X: over_x, GATHER: gather, MASK: make_mask, EXCHANGE: exchange}
    for place, (unit, step) in enumerate(ORDER):
        ring_step(unit, step)
        if place == 3:
            for way in range(2):
                left_v[way] = split_table(tab_v[1 - way, :SPAN, :SPAN], 1)
                right_v[way] = split_table(tab_v[way], 0)
        for task, what in TASKS.get(place, ()):
            tasks[task](what)
    for task, what in TAIL:
        tasks[task](what)

    pltpu.make_async_copy(res, residual.at[0], res_sem).wait()
    pltpu.make_async_copy(upd, update.at[:, z], upd_sem).wait()
    sent(stage, pair_send)
    for direction in (0, 1):
        sent(ring.at[direction], ring_send.at[direction])
    sent(zbuf, z_send)
    sent(xbuf.at[:, pl.ds(0, NX - 1)], x_send)
    for unit in range(len(UNITS)):
        arrived(zbuf.at[UNITS[unit][0], :, :, lanes(unit)], a_recv.at[unit])
    sent(zbuf, a_send)


def shards(grad_parts, momentum, keep_counts, keep_blocks):
    anywhere = pl.BlockSpec(memory_space=pl.ANY)
    outside = pl.BlockSpec(memory_space=pltpu.HBM)
    dma = pltpu.SemaphoreType.DMA
    update, residual = pl.pallas_call(
        kernel,
        out_shape=(
            pltpu.VMEM((CHUNKS, NZ, PIECE, COLS), F32),
            pltpu.VMEM((1, ROWS, COLS), F32),
        ),
        in_specs=[outside] * 5,
        out_specs=(anywhere, anywhere),
        scratch_shapes=[
            pltpu.VMEM((ROWS, WIDE), BF16),
            pltpu.VMEM((ROWS, COLS), F32),
            pltpu.VMEM((CHUNKS, SPANS), jnp.int32),
            pltpu.VMEM((SPANS, CHUNKS, KMAX), jnp.int32),
            pltpu.VMEM((2, 2 * SPAN, 2 * SPAN), F32),
            pltpu.VMEM((2, SPAN, 3 * SPAN), BF16),
            pltpu.VMEM((2, 6 * SPAN, 2 * SPAN), BF16),
            pltpu.VMEM((CHUNKS, NY, SPAN, COLS), F32),
            pltpu.VMEM((CHUNKS, NY, SPAN, COLS), F32),
            pltpu.VMEM((2, CHUNKS, 2, HALF, COLS), F32),
            pltpu.VMEM((2, CHUNKS, STEPS, HALF, COLS), F32),
            pltpu.VMEM((ROWS, COLS), F32),
            pltpu.VMEM((ROWS, COLS), F32),
            pltpu.VMEM((CHUNKS, NZ, PIECE, COLS), F32),
            pltpu.VMEM((CHUNKS, NZ - 1, PIECE, COLS), F32),
            pltpu.VMEM((CHUNKS, NX, PIECE, COLS), F32),
            pltpu.VMEM((CHUNKS, PIECE, COLS), F32),
            dma((CHUNKS + 4,)),
            dma,
            dma,
            dma,
            dma((CHUNKS, NY)),
            dma((2,)),
            dma((2, len(UNITS), STEPS)),
            dma,
            dma((len(UNITS),)),
            dma,
            dma((len(UNITS),)),
            dma,
            dma((len(UNITS),)),
        ],
        compiler_params=pltpu.CompilerParams(
            collective_id=0, has_side_effects=True, vmem_limit_bytes=VMEM_LIMIT
        ),
        cost_estimate=pl.CostEstimate(
            flops=10**9, bytes_accessed=5 * 10**6, transcendentals=0
        ),
    )(grad_parts, momentum, keep_counts, keep_blocks.transpose(0, 2, 1, 3), jnp.asarray(dct_tables()))
    return update.reshape(ROWS, COLS), residual


def solution(mesh):
    return jax.shard_map(
        shards,
        mesh=mesh,
        in_specs=(
            P("rep", "fsdp", None, None),
            P("rep", None, "fsdp"),
            P("rep", None, "fsdp"),
            P("rep", None, "fsdp", None),
        ),
        out_specs=(P(None, "fsdp"), P("rep", None, "fsdp")),
        check_vma=False,
    )
```

```python
import functools

import jax
import jax.numpy as jnp
import numpy as np
from jax import lax
from jax.experimental import pallas as pl
from jax.experimental.pallas import tpu as pltpu
from jax.sharding import PartitionSpec as P

MESH = pl.DeviceIdType.MESH
F32 = jnp.float32
BF16 = jnp.bfloat16

SPAN = 64
GRID = 8
KMAX = 16
NZ, NX, NY, NCORE = 8, 4, 8, 2
ROWS, COLS, WIDE = 256, 384, 6144
CHUNKS = ROWS // SPAN
SPANS = COLS // SPAN
HALF = SPAN // 2
PIECE = SPAN // NZ
STEPS = NY - 1
VMEM_LIMIT = 62 * 2**20
DISTANCES = (4, 3, -3, 2, -2, 1, -1, 0)
SLOT = {d: i for i, d in enumerate(DISTANCES)}
HIGHEST = lax.Precision.HIGHEST
VMEM_LIMIT = 62 * 2**20
UNITS = ((0, 0, 3), (1, 0, 3), (2, 0, 3), (3, 0, 3))
GROUPS = ((2, 0), (2, 1), (2, 2), (3, 0), (3, 1), (3, 2))
NG = len(GROUPS)
SKIP = 2 * GROUPS[0][1]
WIDTH = NG * 128
LISTED = 2 * NG * GRID
HALF_LISTED = LISTED // 2
ROW0 = GROUPS[0][0]
EARLY = tuple(u for u in range(len(UNITS)) if UNITS[u][0] < ROW0)
LATE = tuple(u for u in range(len(UNITS)) if UNITS[u][0] >= ROW0)
EXCHANGE, RING, SPREAD, PLACE, PICK, LIST, MASK, FINISH, OVER_X, GATHER, DECODE, LAST = range(12)
PROGRAM = (
    [(RING, 0, 0), (EXCHANGE, 0, 4, 8), (RING, 0, 1), (EXCHANGE, 1, 0, 8), (RING, 1, 0), (RING, 1, 1)]
    + [(EXCHANGE, 3, 0, 8), (EXCHANGE, 2, 0, 8), (SPREAD,), (RING, 0, 2), (PICK, 4), (RING, 0, 3)]
    + [(LIST, 0), (PICK, 3), (PICK, -3), (RING, 1, 2), (LIST, 1), (RING, 0, 4), (RING, 0, 5)]
    + [(LIST, 2), (RING, 1, 3), (PICK, 2), (PICK, -2), (LIST, 3), (RING, 0, 6), (PICK, 1), (LIST, 4)]
    + [(PICK, -1), (RING, 1, 4), (LIST, 5), (MASK, 0), (RING, 1, 5), (FINISH, 0), (LIST, 6)]
    + [(RING, 1, 6), (RING, 2, 0), (RING, 3, 0), (RING, 2, 1), (RING, 3, 1), (PICK, 0), (PLACE,)]
    + [(DECODE,), (MASK, 1), (FINISH, 1), (RING, 2, 2), (RING, 3, 2), (OVER_X, 0), (RING, 2, 3)]
    + [(RING, 3, 3), (RING, 2, 4), (GATHER, 0), (RING, 3, 4), (OVER_X, 2), (RING, 2, 5)]
    + [(OVER_X, 3), (RING, 3, 5), (RING, 2, 6), (GATHER, 2), (OVER_X, 1), (RING, 3, 6)]
    + [(GATHER, 3), (LAST, 2), (GATHER, 1), (LAST, 3)]
)


def dct_tables():
    k = np.arange(SPAN, dtype=np.float64)[:, None]
    n = np.arange(SPAN, dtype=np.float64)[None, :]
    basis = np.cos(np.pi * (2.0 * n + 1.0) * k / (2.0 * SPAN)) * np.sqrt(2.0 / SPAN)
    basis[0] *= np.sqrt(0.5)
    pair = np.kron(np.eye(2), basis)
    return np.stack([pair.T, pair]).astype(np.float32)


def split_table(table, axis):
    high = table.astype(BF16)
    low = (table - high.astype(F32)).astype(BF16)
    return jnp.concatenate([high, high, low], axis=axis)


def split(values, axis):
    high = values.astype(BF16)
    low = (values - high.astype(F32)).astype(BF16)
    return jnp.concatenate([high, low, high], axis=axis)


def step_distance(direction, step):
    distance = 4 - (step + 1) // 2
    half = (step + direction) % 2
    return (distance if direction == 0 else -distance), half


def kernel(
    grad, momentum, counts, blocks, tables,
    update, residual,
    g_v, m_v, cnt_v, blk_v, tab_v, left_v, right_v,
    tile, tiles, spread_v, place_v, packed, brought, stage, other, first, ring, mask, res, inv, zbuf, xbuf, upd,
    load_sem, res_sem, upd_sem, pair_send, pair_recv, ring_send, ring_recv,
    tile_send, tile_recv, list_send, list_recv, z_send, z_recv, x_send, x_recv, a_send, a_recv,
):
    rep, fsdp = lax.axis_index("rep"), lax.axis_index("fsdp")
    z, x = rep // NX, rep % NX
    y, core = fsdp // NCORE, fsdp % NCORE
    peer = {"fsdp": y * NCORE + 1 - core}

    def at_y(d):
        return {"fsdp": lax.rem(y + d, NY) * NCORE + core}

    neighbours = (at_y(1), at_y(NY - 1))

    def at_z(d):
        return {"rep": lax.rem(z + d, NZ) * NX + x}

    def at_x(d):
        return {"rep": z * NX + lax.rem(x + d, NX)}

    partners = (
        [peer]
        + [at_y(d) for d in range(1, NY)]
        + [at_z(d) for d in range(1, NZ)]
        + [at_x(d) for d in range(1, NX)]
    )

    small = [
        (counts.at[0], cnt_v), (blocks.at[0], blk_v),
        (tables, tab_v), (momentum.at[0], m_v),
    ]
    loads = [
        pltpu.make_async_copy(
            grad.at[0, 0, pl.ds(k * SPAN, SPAN), :],
            g_v.at[pl.ds(k * SPAN, SPAN), :],
            load_sem.at[k],
        )
        for k in range(CHUNKS)
    ] + [
        pltpu.make_async_copy(src, dst, load_sem.at[CHUNKS + i])
        for i, (src, dst) in enumerate(small)
    ]
    for load in loads:
        load.start()

    barrier = pltpu.get_barrier_semaphore()
    for partner in partners:
        pl.semaphore_signal(barrier, inc=1, device_id=partner, device_id_type=MESH)

    def columns(distance, which, first_lane=0, width=COLS):
        target = lax.rem(y + distance + NY, NY) * NCORE + which
        return pl.ds(pl.multiple_of(target * COLS + first_lane, 128), width)

    def lanes(unit):
        _, low, high = UNITS[unit]
        return pl.ds(low * 128, (high - low) * 128)

    def moved(src, dst, send_sem, recv_sem, device):
        return pltpu.make_async_remote_copy(
            src_ref=src, dst_ref=dst, send_sem=send_sem, recv_sem=recv_sem,
            device_id=device, device_id_type=MESH,
        )

    def pair_copy(k, i):
        return moved(stage.at[k, i], other.at[k, i], pair_send, pair_recv.at[k, i], peer)

    def fill_stage(k, i):
        stage[k, i] = g_v[pl.ds(k * SPAN, SPAN), columns(DISTANCES[i], 1 - core)].astype(F32)

    exchanged = set()

    def need(k, distance):
        if (k, distance) not in exchanged:
            exchanged.add((k, distance))
            pair_copy(k, SLOT[distance]).wait_recv()

    def own(unit, distance, half):
        k, low, high = UNITS[unit]
        need(k, distance)
        return (
            g_v[
                pl.ds(k * SPAN + half * HALF, HALF),
                columns(distance, core, low * 128, (high - low) * 128),
            ].astype(F32)
            + other[k, SLOT[distance], pl.ds(half * HALF, HALF), lanes(unit)]
        )

    def ring_copy(direction, unit, step):
        k, window = UNITS[unit][0], lanes(unit)
        return moved(
            first.at[direction, k, step, :, window]
            if step < 2
            else ring.at[direction, k, step - 2, :, window],
            ring.at[direction, k, step, :, window],
            ring_send.at[direction],
            ring_recv.at[direction, unit, step],
            neighbours[direction],
        )

    def ring_step(unit, step):
        k, window = UNITS[unit][0], lanes(unit)
        for direction in (0, 1):
            distance, half = step_distance(direction, step)
            if distance == -4:
                distance = 4
            if step < 2:
                first[direction, k, step, :, window] = own(unit, distance, half)
            else:
                ring_copy(direction, unit, step - 2).wait_recv()
                ring[direction, k, step - 2, :, window] += own(unit, distance, half)
            ring_copy(direction, unit, step).start()

    def places(k):
        spread = jnp.where(
            lax.broadcasted_iota(jnp.int32, (SPANS, COLS), 1) // SPAN
            == lax.broadcasted_iota(jnp.int32, (SPANS, COLS), 0),
            1.0, 0.0,
        ).astype(BF16)
        numbers = lax.dot_general(
            blk_v[:, k, :].astype(F32).astype(BF16), spread, (((0,), (0,)), ((), ())),
            preferred_element_type=F32,
        )
        live = jnp.dot(
            cnt_v[...].astype(F32).astype(BF16), spread, preferred_element_type=F32
        )[k : k + 1, :]
        slot = lax.broadcasted_iota(jnp.int32, (KMAX, COLS), 0).astype(F32)
        column = lax.broadcasted_iota(jnp.int32, (KMAX, COLS), 1)
        place = numbers - ((column % SPAN) // GRID).astype(F32)
        return jnp.where(slot + 0.5 < live, place, -100.0)

    def make_mask(k):
        place = places(k)
        for u in range(GRID):
            hit = jnp.where(place == float(u * GRID), 1.0, 0.0)
            row = jnp.max(hit, axis=0, keepdims=True)
            mask[pl.ds(k * SPAN + u * GRID, GRID), :] = jnp.broadcast_to(row, (GRID, COLS))

    def make_tile():
        span = lax.broadcasted_iota(jnp.int32, (SPANS, 128), 0)
        lane = lax.broadcasted_iota(jnp.int32, (SPANS, 128), 1)
        total = jnp.zeros((GRID, 128), F32)
        for k in range(ROW0, CHUNKS):
            listed = blk_v[:, k, :].astype(F32).astype(BF16)
            at = span + (k - ROW0) * SPANS - SKIP
            for h in range(2):
                chosen = jnp.where((lane == at + 64 * h) & (at >= 0), 1.0, 0.0).astype(BF16)
                moved_out = lax.dot_general(
                    listed, chosen, (((0,), (0,)), ((), ())), preferred_element_type=F32
                )
                total = total + moved_out[h * GRID : (h + 1) * GRID]
        tile[...] = total

    def make_spread():
        lane = lax.broadcasted_iota(jnp.int32, (128, WIDTH), 0)
        span = lax.broadcasted_iota(jnp.int32, (128, WIDTH), 1) // SPAN
        for h in range(2):
            spread_v[h] = jnp.where(lane == span + 64 * h, 1.0, 0.0).astype(BF16)

    def tile_copy(d):
        return moved(tile, tiles.at[d - 1], tile_send, tile_recv, at_y(d))

    def listed_place(distance):
        source = tile[...] if distance == 0 else tiles[7 - distance % NY]
        column = lax.broadcasted_iota(jnp.int32, (GRID, WIDTH), 1)
        group = ((column % SPAN) // GRID).astype(F32)
        return jnp.concatenate(
            [
                jnp.dot(source.astype(BF16), spread_v[h], preferred_element_type=F32) - group
                for h in range(2)
            ],
            axis=0,
        )

    def lane_bit(size):
        lane = lax.broadcasted_iota(jnp.int32, (LISTED, 128), 1)
        return (lane // size) % 2 == 1

    def listed_sum(distance):
        fields = {}
        for k in range(ROW0, CHUNKS):
            rows = pl.ds(k * SPAN, SPAN)
            need(k, distance)
            field = g_v[rows, columns(distance, core)].astype(F32) + other[k, SLOT[distance]]
            if distance == 0:
                field = field + 0.9 * m_v[rows, :]
            fields[k] = field
        field = jnp.concatenate([fields[k][:, g * 128 : (g + 1) * 128] for k, g in GROUPS], axis=1)
        coeff = transform(field, 0)
        place = listed_place(distance)
        picked = []
        for slot in range(KMAX):
            where = jnp.broadcast_to(place[slot : slot + 1, :], (GRID, WIDTH))
            got = jnp.zeros((GRID, WIDTH), F32)
            for u in range(GRID):
                got = jnp.where(where == float(u * GRID), coeff[u * GRID : (u + 1) * GRID], got)
            picked.append(got)
        values = [
            jnp.concatenate(
                [
                    picked[h * GRID + j][:, g * 128 : (g + 1) * 128]
                    for h in range(2)
                    for g in range(NG)
                ],
                axis=0,
            )
            for j in range(GRID)
        ]
        for size in (32, 16, 8):
            bit = lane_bit(size)
            half = len(values) // 2
            merged = []
            for j in range(half):
                low, high = values[j], values[j + half]
                out = jnp.where(bit, low, high)
                out = jnp.where(bit, pltpu.roll(out, size, 1), pltpu.roll(out, 128 - size, 1))
                merged.append(jnp.where(bit, high, low) + out)
            values = merged
        packed[SLOT[distance]] = values[0]

    def half_rows(half):
        return pl.ds(half * HALF_LISTED, HALF_LISTED)

    def list_copy(direction, step):
        if step < 2:
            distance, half = step_distance(direction, step)
            source = packed.at[SLOT[4 if distance == -4 else distance], half_rows(half)]
        else:
            source = brought.at[direction, step - 2]
        return moved(
            source, brought.at[direction, step],
            list_send.at[direction], list_recv.at[direction, step], neighbours[direction],
        )

    def list_step(step):
        for direction in (0, 1):
            distance, half = step_distance(direction, step)
            if step >= 2:
                list_copy(direction, step - 2).wait_recv()
                brought[direction, step - 2] += packed[SLOT[distance], half_rows(half)]
            list_copy(direction, step).start()

    def decode():
        for step in (STEPS - 2, STEPS - 1):
            for direction in (0, 1):
                list_copy(direction, step).wait_recv()
        own_part = packed[SLOT[0]]
        values = [
            own_part
            + jnp.concatenate(
                [
                    brought[0, STEPS - 1] + brought[1, STEPS - 2],
                    brought[0, STEPS - 2] + brought[1, STEPS - 1],
                ],
                axis=0,
            )
        ]
        for size in (8, 16, 32):
            bit = lane_bit(size)
            low, high = [], []
            for value in values:
                low.append(jnp.where(bit, pltpu.roll(value, size, 1), value))
                high.append(jnp.where(bit, value, pltpu.roll(value, 128 - size, 1)))
            values = low + high
        place = jnp.concatenate(
            [place_v[k - ROW0][:, g * 128 : (g + 1) * 128] for k, g in GROUPS], axis=1
        )
        kept = [jnp.zeros((GRID, WIDTH), F32)] * GRID
        for slot in range(KMAX):
            h, j = slot // GRID, slot % GRID
            at = [(h * NG + g) * GRID for g in range(NG)]
            value = jnp.concatenate([values[j][r : r + GRID] for r in at], axis=1)
            where = jnp.broadcast_to(place[slot : slot + 1, :], (GRID, WIDTH))
            kept = [
                jnp.where(where == float(u * GRID), value, kept[u]) for u in range(GRID)
            ]
        decoded = transform(jnp.concatenate(kept, axis=0), 1)
        for i, (k, g) in enumerate(GROUPS):
            window = pl.ds(g * 128, 128)
            inv[k, :, :, window] = decoded[:, i * 128 : (i + 1) * 128].reshape(NZ, PIECE, 128)
        for unit in LATE:
            for d in (4, 3, 5, 2, 6, 1, 7):
                z_copy(unit, d).start()

    def transform(values, way):
        groups = values.shape[1] // 128
        rows = jnp.dot(left_v[way], split(values, 0), preferred_element_type=F32)
        parts = jnp.concatenate([rows[:, g * 128 : (g + 1) * 128] for g in range(groups)], axis=0)
        done = jnp.dot(split(parts, 1), right_v[way], preferred_element_type=F32)
        return jnp.concatenate([done[g * SPAN : (g + 1) * SPAN] for g in range(groups)], axis=1)

    def z_copy(unit, d):
        k, window = UNITS[unit][0], lanes(unit)
        return moved(
            inv.at[k, lax.rem(z + d, NZ), :, window], zbuf.at[k, d - 1, :, window],
            z_send, z_recv.at[unit], at_z(d),
        )

    def x_copy(unit, d):
        k, window = UNITS[unit][0], lanes(unit)
        return moved(
            xbuf.at[k, x, :, window], xbuf.at[k, x, :, window],
            x_send, x_recv.at[unit], at_x(d),
        )

    def a_copy(unit, d):
        k, window = UNITS[unit][0], lanes(unit)
        return moved(
            upd.at[k, :, window], update.at[k, z, :, window],
            a_send, a_recv.at[unit], at_z(d),
        )

    def arrived(ref, sem):
        moved(ref, ref, z_send, sem, peer).wait_recv()

    def sent(ref, sem):
        moved(ref, ref, sem, z_recv.at[0], peer).wait_send()

    def residual_copy(unit):
        rows, window = pl.ds(UNITS[unit][0] * SPAN, SPAN), lanes(unit)
        return pltpu.make_async_copy(res.at[rows, window], residual.at[0, rows, window], res_sem)

    def update_copy(unit):
        k, window = UNITS[unit][0], lanes(unit)
        return pltpu.make_async_copy(upd.at[k, :, window], update.at[k, z, :, window], upd_sem)

    def summed(unit):
        k, window = UNITS[unit][0], lanes(unit)
        for step in (STEPS - 2, STEPS - 1):
            for direction in (0, 1):
                ring_copy(direction, unit, step).wait_recv()
        lower = (
            own(unit, 0, 0) + ring[0, k, STEPS - 1, :, window] + ring[1, k, STEPS - 2, :, window]
        )
        upper = (
            own(unit, 0, 1) + ring[0, k, STEPS - 2, :, window] + ring[1, k, STEPS - 1, :, window]
        )
        rows = pl.ds(k * SPAN, SPAN)
        return 0.9 * m_v[rows, window] + jnp.concatenate([lower, upper], axis=0)

    def finish(unit):
        k, window = UNITS[unit][0], lanes(unit)
        rows = pl.ds(k * SPAN, SPAN)
        fresh = summed(unit)
        decoded = transform(transform(fresh, 0) * mask[rows, window], 1)
        inv[k, :, :, window] = decoded.reshape(NZ, PIECE, decoded.shape[1])
        for d in (4, 3, 5, 2, 6, 1, 7):
            z_copy(unit, d).start()
        res[rows, window] = fresh - decoded
        residual_copy(unit).start()

    def last(unit):
        k, window = UNITS[unit][0], lanes(unit)
        rows = pl.ds(k * SPAN, SPAN)
        res[rows, window] = summed(unit) - inv[k, :, :, window].reshape(SPAN, COLS)
        residual_copy(unit).start()

    def over_x(unit):
        k, window = UNITS[unit][0], lanes(unit)
        arrived(zbuf.at[k, :, :, window], z_recv.at[unit])
        xbuf[k, x, :, window] = inv[k, z, :, window] + jnp.sum(zbuf[k, :, :, window], axis=0)
        for d in (2, 1, 3):
            x_copy(unit, d).start()

    def gather(unit):
        k, window = UNITS[unit][0], lanes(unit)
        arrived(xbuf.at[k, pl.ds(0, NX - 1), :, window], x_recv.at[unit])
        total = (xbuf[k, 0, :, window] + xbuf[k, 1, :, window]) + (
            xbuf[k, 2, :, window] + xbuf[k, 3, :, window]
        )
        upd[k, :, window] = total * (1.0 / (NZ * NX))
        for d in (4, 3, 5, 2, 6, 1, 7):
            a_copy(unit, d).start()
        update_copy(unit).start()

    def exchange(k, begin, end):
        if k > 1:
            for i in range(begin, end):
                fill_stage(k, i)
        for i in range(begin, end):
            pair_copy(k, i).start()

    def spread_tables():
        for way in range(2):
            left_v[way] = split_table(tab_v[1 - way, :SPAN, :SPAN], 1)
            right_v[way] = split_table(tab_v[way], 0)
        make_spread()
        arrived(tiles, tile_recv)

    def late_places():
        for k in range(ROW0, CHUNKS):
            place_v[k - ROW0] = places(k)

    for load in loads[CHUNKS : CHUNKS + 2]:
        load.wait()
    make_tile()
    for k in range(2):
        loads[k].wait()
        for i in range(NY):
            fill_stage(k, i)
    pl.semaphore_wait(barrier, len(partners))
    exchange(0, 0, 4)
    for d in (4, 3, 5, 2, 6, 1, 7):
        tile_copy(d).start()
    for load in loads[2:CHUNKS] + loads[CHUNKS + 2 :]:
        load.wait()

    tasks = {
        EXCHANGE: exchange, RING: ring_step, SPREAD: spread_tables, PLACE: late_places,
        PICK: listed_sum, LIST: list_step,
        MASK: make_mask, FINISH: finish, OVER_X: over_x, GATHER: gather, DECODE: decode, LAST: last,
    }
    for task, *what in PROGRAM:
        tasks[task](*what)

    pltpu.make_async_copy(res, residual.at[0], res_sem).wait()
    pltpu.make_async_copy(upd, update.at[:, z], upd_sem).wait()
    sent(stage, pair_send)
    sent(tiles, tile_send)
    for direction in (0, 1):
        sent(ring.at[direction], ring_send.at[direction])
        sent(brought.at[direction], list_send.at[direction])
    sent(zbuf, z_send)
    sent(xbuf.at[:, pl.ds(0, NX - 1)], x_send)
    for unit in range(len(UNITS)):
        arrived(zbuf.at[UNITS[unit][0], :, :, lanes(unit)], a_recv.at[unit])
    sent(zbuf, a_send)


def shards(grad_parts, momentum, keep_counts, keep_blocks):
    anywhere = pl.BlockSpec(memory_space=pl.ANY)
    outside = pl.BlockSpec(memory_space=pltpu.HBM)
    dma = pltpu.SemaphoreType.DMA
    update, residual = pl.pallas_call(
        kernel,
        out_shape=(
            pltpu.VMEM((CHUNKS, NZ, PIECE, COLS), F32),
            pltpu.VMEM((1, ROWS, COLS), F32),
        ),
        in_specs=[outside] * 5,
        out_specs=(anywhere, anywhere),
        scratch_shapes=[
            pltpu.VMEM((ROWS, WIDE), BF16),
            pltpu.VMEM((ROWS, COLS), F32),
            pltpu.VMEM((CHUNKS, SPANS), jnp.int32),
            pltpu.VMEM((SPANS, CHUNKS, KMAX), jnp.int32),
            pltpu.VMEM((2, 2 * SPAN, 2 * SPAN), F32),
            pltpu.VMEM((2, SPAN, 3 * SPAN), BF16),
            pltpu.VMEM((2, 6 * SPAN, 2 * SPAN), BF16),
            pltpu.VMEM((GRID, 128), F32),
            pltpu.VMEM((NY - 1, GRID, 128), F32),
            pltpu.VMEM((2, 128, WIDTH), BF16),
            pltpu.VMEM((CHUNKS - ROW0, KMAX, COLS), F32),
            pltpu.VMEM((NY, LISTED, 128), F32),
            pltpu.VMEM((2, STEPS, HALF_LISTED, 128), F32),
            pltpu.VMEM((CHUNKS, NY, SPAN, COLS), F32),
            pltpu.VMEM((CHUNKS, NY, SPAN, COLS), F32),
            pltpu.VMEM((2, CHUNKS, 2, HALF, COLS), F32),
            pltpu.VMEM((2, CHUNKS, STEPS, HALF, COLS), F32),
            pltpu.VMEM((ROWS, COLS), F32),
            pltpu.VMEM((ROWS, COLS), F32),
            pltpu.VMEM((CHUNKS, NZ, PIECE, COLS), F32),
            pltpu.VMEM((CHUNKS, NZ - 1, PIECE, COLS), F32),
            pltpu.VMEM((CHUNKS, NX, PIECE, COLS), F32),
            pltpu.VMEM((CHUNKS, PIECE, COLS), F32),
            dma((CHUNKS + 4,)),
            dma,
            dma,
            dma,
            dma((CHUNKS, NY)),
            dma((2,)),
            dma((2, len(UNITS), STEPS)),
            dma,
            dma,
            dma((2,)),
            dma((2, STEPS)),
            dma,
            dma((len(UNITS),)),
            dma,
            dma((len(UNITS),)),
            dma,
            dma((len(UNITS),)),
        ],
        compiler_params=pltpu.CompilerParams(
            collective_id=0, has_side_effects=True, vmem_limit_bytes=VMEM_LIMIT
        ),
        cost_estimate=pl.CostEstimate(
            flops=10**9, bytes_accessed=5 * 10**6, transcendentals=0
        ),
    )(grad_parts, momentum, keep_counts, keep_blocks.transpose(0, 2, 1, 3), jnp.asarray(dct_tables()))
    return update.reshape(ROWS, COLS), residual


def solution(mesh):
    return jax.shard_map(
        shards,
        mesh=mesh,
        in_specs=(
            P("rep", "fsdp", None, None),
            P("rep", None, "fsdp"),
            P("rep", None, "fsdp"),
            P("rep", None, "fsdp", None),
        ),
        out_specs=(P(None, "fsdp"), P("rep", None, "fsdp")),
        check_vma=False,
    )
```

```python
import functools

import jax
import jax.numpy as jnp
import numpy as np
from jax import lax
from jax.experimental import pallas as pl
from jax.experimental.pallas import tpu as pltpu
from jax.sharding import PartitionSpec as P

MESH = pl.DeviceIdType.MESH
F32 = jnp.float32
BF16 = jnp.bfloat16

SPAN = 64
GRID = 8
KMAX = 16
NZ, NX, NY, NCORE = 8, 4, 8, 2
ROWS, COLS, WIDE = 256, 384, 6144
CHUNKS = ROWS // SPAN
SPANS = COLS // SPAN
HALF = SPAN // 2
PIECE = SPAN // NZ
STEPS = NY - 1
VMEM_LIMIT = 62 * 2**20
DISTANCES = (4, 3, -3, 2, -2, 1, -1, 0)
SLOT = {d: i for i, d in enumerate(DISTANCES)}
HIGHEST = lax.Precision.HIGHEST
VMEM_LIMIT = 62 * 2**20
UNITS = ((0, 0, 3), (1, 0, 2), (1, 2, 3), (2, 0, 3), (3, 0, 3))
GROUPS = ((2, 0), (2, 1), (2, 2), (3, 0), (3, 1), (3, 2))
NG = len(GROUPS)
SKIP = 2 * GROUPS[0][1]
WIDTH = NG * 128
LISTED = 2 * NG * GRID
HALF_LISTED = LISTED // 2
ROW0 = GROUPS[0][0]
LATE = tuple(u for u in range(len(UNITS)) if UNITS[u][0] >= ROW0)
EXCHANGE, RING, SPREAD, PLACE, PICK, LIST, MASK, FINISH, OVER_X, GATHER, DECODE, LAST = range(12)
PROGRAM = (
    [(RING, 0, 0), (EXCHANGE, 0, 3, 8), (RING, 0, 1), (EXCHANGE, 1, 0, 8), (RING, 1, 0), (RING, 1, 1)]
    + [(RING, 2, 0), (RING, 2, 1), (EXCHANGE, 3, 0, 8), (EXCHANGE, 2, 0, 8), (SPREAD,), (RING, 0, 2)]
    + [(PICK, 4), (RING, 0, 3), (LIST, 0), (PICK, 3), (PICK, -3), (LIST, 1), (LIST, 2), (RING, 0, 4)]
    + [(RING, 0, 5), (RING, 1, 2), (PICK, 2), (PICK, -2), (LIST, 3), (LIST, 4), (RING, 0, 6)]
    + [(RING, 1, 3), (RING, 2, 2), (PICK, 1), (PICK, -1), (LIST, 5), (LIST, 6), (RING, 2, 3)]
    + [(MASK, 0), (RING, 1, 4), (FINISH, 0), (RING, 1, 5), (RING, 2, 4), (RING, 3, 0), (PICK, 0), (PLACE,)]
    + [(DECODE,), (RING, 4, 0), (RING, 1, 6), (RING, 2, 5), (RING, 2, 6), (RING, 3, 1), (RING, 4, 1)]
    + [(MASK, 1), (RING, 3, 2), (RING, 4, 2), (FINISH, 1), (FINISH, 2), (OVER_X, 0), (RING, 3, 3)]
    + [(RING, 4, 3), (OVER_X, 3), (RING, 3, 4), (RING, 4, 4), (OVER_X, 4), (GATHER, 0), (RING, 3, 5)]
    + [(RING, 4, 5), (GATHER, 3), (OVER_X, 1), (OVER_X, 2), (RING, 3, 6), (RING, 4, 6)]
    + [(GATHER, 4), (GATHER, 1), (GATHER, 2), (LAST, 3), (LAST, 4)]
)


def dct_tables():
    k = np.arange(SPAN, dtype=np.float64)[:, None]
    n = np.arange(SPAN, dtype=np.float64)[None, :]
    basis = np.cos(np.pi * (2.0 * n + 1.0) * k / (2.0 * SPAN)) * np.sqrt(2.0 / SPAN)
    basis[0] *= np.sqrt(0.5)
    pair = np.kron(np.eye(2), basis)
    return np.stack([pair.T, pair]).astype(np.float32)


def split_table(table, axis):
    high = table.astype(BF16)
    low = (table - high.astype(F32)).astype(BF16)
    return jnp.concatenate([high, high, low], axis=axis)


def split(values, axis):
    high = values.astype(BF16)
    low = (values - high.astype(F32)).astype(BF16)
    return jnp.concatenate([high, low, high], axis=axis)


def step_distance(direction, step):
    distance = 4 - (step + 1) // 2
    half = (step + direction) % 2
    return (distance if direction == 0 else -distance), half


def kernel(
    grad, momentum, counts, blocks, tables,
    update, residual,
    g_v, m_v, cnt_v, blk_v, tab_v, left_v, right_v,
    tile, tiles, spread_v, place_v, packed, brought, stage, other, first, ring, mask, res, inv, zbuf, xbuf, upd,
    load_sem, res_sem, upd_sem, pair_send, pair_recv, ring_send, ring_recv,
    tile_send, tile_recv, list_send, list_recv, z_send, z_recv, x_send, x_recv, a_send, a_recv,
):
    rep, fsdp = lax.axis_index("rep"), lax.axis_index("fsdp")
    z, x = rep // NX, rep % NX
    y, core = fsdp // NCORE, fsdp % NCORE
    peer = {"fsdp": y * NCORE + 1 - core}

    def at_y(d):
        return {"fsdp": lax.rem(y + d, NY) * NCORE + core}

    neighbours = (at_y(1), at_y(NY - 1))

    def at_z(d):
        return {"rep": lax.rem(z + d, NZ) * NX + x}

    def at_x(d):
        return {"rep": z * NX + lax.rem(x + d, NX)}

    partners = (
        [at_z(d) for d in (4, 3, 5, 2, 6, 1, 7)]
        + [at_x(d) for d in (2, 1, 3)]
        + [at_y(d) for d in (4, 3, 5, 2, 6, 1, 7)]
        + [peer]
    )

    barrier = pltpu.get_barrier_semaphore()
    for partner in partners:
        pl.semaphore_signal(barrier, inc=1, device_id=partner, device_id_type=MESH)

    small = [
        (counts.at[0], cnt_v), (blocks.at[0], blk_v),
        (tables, tab_v), (momentum.at[0], m_v),
    ]
    loads = [
        pltpu.make_async_copy(
            grad.at[0, 0, pl.ds(k * SPAN, SPAN), :],
            g_v.at[pl.ds(k * SPAN, SPAN), :],
            load_sem.at[k],
        )
        for k in range(CHUNKS)
    ] + [
        pltpu.make_async_copy(src, dst, load_sem.at[CHUNKS + i])
        for i, (src, dst) in enumerate(small)
    ]
    for i in (0, CHUNKS + 1, 1, CHUNKS, CHUNKS + 2, CHUNKS + 3, 3, 2):
        loads[i].start()

    def columns(distance, which, first_lane=0, width=COLS):
        target = lax.rem(y + distance + NY, NY) * NCORE + which
        return pl.ds(pl.multiple_of(target * COLS + first_lane, 128), width)

    def lanes(unit):
        _, low, high = UNITS[unit]
        return pl.ds(low * 128, (high - low) * 128)

    def moved(src, dst, send_sem, recv_sem, device):
        return pltpu.make_async_remote_copy(
            src_ref=src, dst_ref=dst, send_sem=send_sem, recv_sem=recv_sem,
            device_id=device, device_id_type=MESH,
        )

    def pair_copy(k, i):
        return moved(stage.at[k, i], other.at[k, i], pair_send, pair_recv.at[k, i], peer)

    def fill_stage(k, i):
        stage[k, i] = g_v[pl.ds(k * SPAN, SPAN), columns(DISTANCES[i], 1 - core)].astype(F32)

    exchanged = set()

    def need(k, distance):
        if (k, distance) not in exchanged:
            exchanged.add((k, distance))
            pair_copy(k, SLOT[distance]).wait_recv()

    def own(unit, distance, half):
        k, low, high = UNITS[unit]
        need(k, distance)
        return (
            g_v[
                pl.ds(k * SPAN + half * HALF, HALF),
                columns(distance, core, low * 128, (high - low) * 128),
            ].astype(F32)
            + other[k, SLOT[distance], pl.ds(half * HALF, HALF), lanes(unit)]
        )

    def ring_copy(direction, unit, step):
        k, window = UNITS[unit][0], lanes(unit)
        return moved(
            first.at[direction, k, step, :, window]
            if step < 2
            else ring.at[direction, k, step - 2, :, window],
            ring.at[direction, k, step, :, window],
            ring_send.at[direction],
            ring_recv.at[direction, unit, step],
            neighbours[direction],
        )

    def ring_step(unit, step):
        k, window = UNITS[unit][0], lanes(unit)
        for direction in (0, 1):
            distance, half = step_distance(direction, step)
            if distance == -4:
                distance = 4
            if step < 2:
                first[direction, k, step, :, window] = own(unit, distance, half)
            else:
                ring_copy(direction, unit, step - 2).wait_recv()
                ring[direction, k, step - 2, :, window] += own(unit, distance, half)
            ring_copy(direction, unit, step).start()

    def places(k):
        spread = jnp.where(
            lax.broadcasted_iota(jnp.int32, (SPANS, COLS), 1) // SPAN
            == lax.broadcasted_iota(jnp.int32, (SPANS, COLS), 0),
            1.0, 0.0,
        ).astype(BF16)
        numbers = lax.dot_general(
            blk_v[:, k, :].astype(F32).astype(BF16), spread, (((0,), (0,)), ((), ())),
            preferred_element_type=F32,
        )
        live = jnp.dot(
            cnt_v[...].astype(F32).astype(BF16), spread, preferred_element_type=F32
        )[k : k + 1, :]
        slot = lax.broadcasted_iota(jnp.int32, (KMAX, COLS), 0).astype(F32)
        column = lax.broadcasted_iota(jnp.int32, (KMAX, COLS), 1)
        place = numbers - ((column % SPAN) // GRID).astype(F32)
        return jnp.where(slot + 0.5 < live, place, -100.0)

    def make_mask(k):
        place = places(k)
        for u in range(GRID):
            hit = jnp.where(place == float(u * GRID), 1.0, 0.0)
            row = jnp.max(hit, axis=0, keepdims=True)
            mask[pl.ds(k * SPAN + u * GRID, GRID), :] = jnp.broadcast_to(row, (GRID, COLS))

    def make_tile():
        span = lax.broadcasted_iota(jnp.int32, (SPANS, 128), 0)
        lane = lax.broadcasted_iota(jnp.int32, (SPANS, 128), 1)
        total = jnp.zeros((GRID, 128), F32)
        for k in range(ROW0, CHUNKS):
            listed = blk_v[:, k, :].astype(F32).astype(BF16)
            at = span + (k - ROW0) * SPANS - SKIP
            for h in range(2):
                chosen = jnp.where((lane == at + 64 * h) & (at >= 0), 1.0, 0.0).astype(BF16)
                moved_out = lax.dot_general(
                    listed, chosen, (((0,), (0,)), ((), ())), preferred_element_type=F32
                )
                total = total + moved_out[h * GRID : (h + 1) * GRID]
        tile[...] = total

    def make_spread():
        lane = lax.broadcasted_iota(jnp.int32, (128, WIDTH), 0)
        span = lax.broadcasted_iota(jnp.int32, (128, WIDTH), 1) // SPAN
        for h in range(2):
            spread_v[h] = jnp.where(lane == span + 64 * h, 1.0, 0.0).astype(BF16)

    def tile_copy(d):
        return moved(tile, tiles.at[d - 1], tile_send, tile_recv, at_y(d))

    def listed_place(distance):
        source = tile[...] if distance == 0 else tiles[7 - distance % NY]
        column = lax.broadcasted_iota(jnp.int32, (GRID, WIDTH), 1)
        group = ((column % SPAN) // GRID).astype(F32)
        return jnp.concatenate(
            [
                jnp.dot(source.astype(BF16), spread_v[h], preferred_element_type=F32) - group
                for h in range(2)
            ],
            axis=0,
        )

    def lane_bit(size):
        lane = lax.broadcasted_iota(jnp.int32, (LISTED, 128), 1)
        return (lane // size) % 2 == 1

    def listed_sum(distance):
        fields = {}
        for k in range(ROW0, CHUNKS):
            rows = pl.ds(k * SPAN, SPAN)
            need(k, distance)
            field = g_v[rows, columns(distance, core)].astype(F32) + other[k, SLOT[distance]]
            if distance == 0:
                field = field + 0.9 * m_v[rows, :]
            fields[k] = field
        field = jnp.concatenate([fields[k][:, g * 128 : (g + 1) * 128] for k, g in GROUPS], axis=1)
        coeff = transform(field, 0)
        place = listed_place(distance)
        picked = []
        for slot in range(KMAX):
            where = jnp.broadcast_to(place[slot : slot + 1, :], (GRID, WIDTH))
            got = jnp.zeros((GRID, WIDTH), F32)
            for u in range(GRID):
                got = jnp.where(where == float(u * GRID), coeff[u * GRID : (u + 1) * GRID], got)
            picked.append(got)
        values = [
            jnp.concatenate(
                [
                    picked[h * GRID + j][:, g * 128 : (g + 1) * 128]
                    for h in range(2)
                    for g in range(NG)
                ],
                axis=0,
            )
            for j in range(GRID)
        ]
        for size in (32, 16, 8):
            bit = lane_bit(size)
            half = len(values) // 2
            merged = []
            for j in range(half):
                low, high = values[j], values[j + half]
                out = jnp.where(bit, low, high)
                out = jnp.where(bit, pltpu.roll(out, size, 1), pltpu.roll(out, 128 - size, 1))
                merged.append(jnp.where(bit, high, low) + out)
            values = merged
        packed[SLOT[distance]] = values[0]

    def half_rows(half):
        return pl.ds(half * HALF_LISTED, HALF_LISTED)

    def list_copy(direction, step):
        if step < 3:
            distance, half = step_distance(direction, step)
            source = packed.at[SLOT[4 if distance == -4 else distance], half_rows(half)]
        else:
            source = brought.at[direction, step - 2]
        return moved(
            source, brought.at[direction, step],
            list_send.at[direction], list_recv.at[direction, step],
            at_y((2, NY - 2)[direction]) if step == 0 else neighbours[direction],
        )

    def list_step(step):
        for direction in (0, 1):
            distance, half = step_distance(direction, step)
            if step >= 3:
                list_copy(direction, step - 2).wait_recv()
                more = packed[SLOT[distance], half_rows(half)]
                if step == 4:
                    list_copy(direction, 0).wait_recv()
                    more = more + brought[direction, 0]
                brought[direction, step - 2] += more
            list_copy(direction, step).start()

    def decode():
        for step in (STEPS - 2, STEPS - 1):
            for direction in (0, 1):
                list_copy(direction, step).wait_recv()
        own_part = packed[SLOT[0]]
        values = [
            own_part
            + jnp.concatenate(
                [
                    brought[0, STEPS - 1] + brought[1, STEPS - 2],
                    brought[0, STEPS - 2] + brought[1, STEPS - 1],
                ],
                axis=0,
            )
        ]
        for size in (8, 16, 32):
            bit = lane_bit(size)
            low, high = [], []
            for value in values:
                low.append(jnp.where(bit, pltpu.roll(value, size, 1), value))
                high.append(jnp.where(bit, value, pltpu.roll(value, 128 - size, 1)))
            values = low + high
        place = jnp.concatenate(
            [place_v[k - ROW0][:, g * 128 : (g + 1) * 128] for k, g in GROUPS], axis=1
        )
        kept = [jnp.zeros((GRID, WIDTH), F32)] * GRID
        for slot in range(KMAX):
            h, j = slot // GRID, slot % GRID
            at = [(h * NG + g) * GRID for g in range(NG)]
            value = jnp.concatenate([values[j][r : r + GRID] for r in at], axis=1)
            where = jnp.broadcast_to(place[slot : slot + 1, :], (GRID, WIDTH))
            kept = [
                jnp.where(where == float(u * GRID), value, kept[u]) for u in range(GRID)
            ]
        decoded = transform(jnp.concatenate(kept, axis=0), 1)
        for i, (k, g) in enumerate(GROUPS):
            window = pl.ds(g * 128, 128)
            inv[k, :, :, window] = decoded[:, i * 128 : (i + 1) * 128].reshape(NZ, PIECE, 128)
        for unit in LATE:
            for d in (4, 3, 5, 2, 6, 1, 7):
                z_copy(unit, d).start()

    def transform(values, way):
        groups = values.shape[1] // 128
        rows = jnp.dot(left_v[way], split(values, 0), preferred_element_type=F32)
        parts = jnp.concatenate([rows[:, g * 128 : (g + 1) * 128] for g in range(groups)], axis=0)
        done = jnp.dot(split(parts, 1), right_v[way], preferred_element_type=F32)
        return jnp.concatenate([done[g * SPAN : (g + 1) * SPAN] for g in range(groups)], axis=1)

    def z_copy(unit, d):
        k, window = UNITS[unit][0], lanes(unit)
        return moved(
            inv.at[k, lax.rem(z + d, NZ), :, window], zbuf.at[k, d - 1, :, window],
            z_send, z_recv.at[unit], at_z(d),
        )

    def x_copy(unit, d):
        k, window = UNITS[unit][0], lanes(unit)
        return moved(
            xbuf.at[k, x, :, window], xbuf.at[k, x, :, window],
            x_send, x_recv.at[unit], at_x(d),
        )

    def a_copy(unit, d):
        k, window = UNITS[unit][0], lanes(unit)
        return moved(
            upd.at[k, :, window], update.at[k, z, :, window],
            a_send, a_recv.at[unit], at_z(d),
        )

    def arrived(ref, sem):
        moved(ref, ref, z_send, sem, peer).wait_recv()

    def sent(ref, sem):
        moved(ref, ref, sem, z_recv.at[0], peer).wait_send()

    def residual_copy(unit):
        rows, window = pl.ds(UNITS[unit][0] * SPAN, SPAN), lanes(unit)
        return pltpu.make_async_copy(res.at[rows, window], residual.at[0, rows, window], res_sem)

    def update_copy(unit):
        k, window = UNITS[unit][0], lanes(unit)
        return pltpu.make_async_copy(upd.at[k, :, window], update.at[k, z, :, window], upd_sem)

    def summed(unit):
        k, window = UNITS[unit][0], lanes(unit)
        for step in (STEPS - 2, STEPS - 1):
            for direction in (0, 1):
                ring_copy(direction, unit, step).wait_recv()
        lower = (
            own(unit, 0, 0) + ring[0, k, STEPS - 1, :, window] + ring[1, k, STEPS - 2, :, window]
        )
        upper = (
            own(unit, 0, 1) + ring[0, k, STEPS - 2, :, window] + ring[1, k, STEPS - 1, :, window]
        )
        rows = pl.ds(k * SPAN, SPAN)
        return 0.9 * m_v[rows, window] + jnp.concatenate([lower, upper], axis=0)

    def finish(unit):
        k, window = UNITS[unit][0], lanes(unit)
        rows = pl.ds(k * SPAN, SPAN)
        fresh = summed(unit)
        decoded = transform(transform(fresh, 0) * mask[rows, window], 1)
        inv[k, :, :, window] = decoded.reshape(NZ, PIECE, decoded.shape[1])
        for d in (4, 3, 5, 2, 6, 1, 7):
            z_copy(unit, d).start()
        res[rows, window] = fresh - decoded
        residual_copy(unit).start()

    def last(unit):
        k, window = UNITS[unit][0], lanes(unit)
        rows = pl.ds(k * SPAN, SPAN)
        res[rows, window] = summed(unit) - inv[k, :, :, window].reshape(SPAN, COLS)
        residual_copy(unit).start()

    def over_x(unit):
        k, window = UNITS[unit][0], lanes(unit)
        arrived(zbuf.at[k, :, :, window], z_recv.at[unit])
        xbuf[k, x, :, window] = inv[k, z, :, window] + jnp.sum(zbuf[k, :, :, window], axis=0)
        for d in (2, 1, 3):
            x_copy(unit, d).start()

    def gather(unit):
        k, window = UNITS[unit][0], lanes(unit)
        arrived(xbuf.at[k, pl.ds(0, NX - 1), :, window], x_recv.at[unit])
        total = (xbuf[k, 0, :, window] + xbuf[k, 1, :, window]) + (
            xbuf[k, 2, :, window] + xbuf[k, 3, :, window]
        )
        upd[k, :, window] = total * (1.0 / (NZ * NX))
        for d in (4, 3, 5, 2, 6, 1, 7):
            a_copy(unit, d).start()
        update_copy(unit).start()

    def exchange(k, begin, end):
        if k > 0:
            loads[k].wait()
            for i in range(begin, end):
                fill_stage(k, i)
        for i in range(begin, end):
            pair_copy(k, i).start()

    def spread_tables():
        for i in (CHUNKS, CHUNKS + 2, CHUNKS + 3):
            loads[i].wait()
        for way in range(2):
            left_v[way] = split_table(tab_v[1 - way, :SPAN, :SPAN], 1)
            right_v[way] = split_table(tab_v[way], 0)
        make_spread()
        arrived(tiles, tile_recv)

    def late_places():
        for k in range(ROW0, CHUNKS):
            place_v[k - ROW0] = places(k)

    loads[0].wait()
    for i in range(NY):
        fill_stage(0, i)
    loads[CHUNKS + 1].wait()
    make_tile()
    pl.semaphore_wait(barrier, len(partners))
    exchange(0, 0, 3)
    for d in (4, 3, 5, 2, 6, 1, 7):
        tile_copy(d).start()

    tasks = {
        EXCHANGE: exchange, RING: ring_step, SPREAD: spread_tables, PLACE: late_places,
        PICK: listed_sum, LIST: list_step,
        MASK: make_mask, FINISH: finish, OVER_X: over_x, GATHER: gather, DECODE: decode, LAST: last,
    }
    for task, *what in PROGRAM:
        tasks[task](*what)

    pltpu.make_async_copy(res, residual.at[0], res_sem).wait()
    pltpu.make_async_copy(upd, update.at[:, z], upd_sem).wait()
    sent(stage, pair_send)
    sent(tiles, tile_send)
    for direction in (0, 1):
        sent(ring.at[direction], ring_send.at[direction])
        sent(brought.at[direction], list_send.at[direction])
    sent(zbuf, z_send)
    sent(xbuf.at[:, pl.ds(0, NX - 1)], x_send)
    for unit in range(len(UNITS)):
        arrived(zbuf.at[UNITS[unit][0], :, :, lanes(unit)], a_recv.at[unit])
    sent(zbuf, a_send)


def put_out(update, residual, update_out, residual_out, sems):
    copies = [
        pltpu.make_async_copy(update, update_out, sems.at[0]),
        pltpu.make_async_copy(residual, residual_out, sems.at[1]),
    ]
    for copy in copies:
        copy.start()
    for copy in copies:
        copy.wait()


def shards(grad_parts, momentum, keep_counts, keep_blocks):
    anywhere = pl.BlockSpec(memory_space=pl.ANY)
    outside = pl.BlockSpec(memory_space=pltpu.HBM)
    dma = pltpu.SemaphoreType.DMA
    update, residual = pl.pallas_call(
        kernel,
        out_shape=(
            pltpu.VMEM((CHUNKS, NZ, PIECE, COLS), F32),
            pltpu.VMEM((1, ROWS, COLS), F32),
        ),
        in_specs=[outside] * 5,
        out_specs=(anywhere, anywhere),
        scratch_shapes=[
            pltpu.VMEM((ROWS, WIDE), BF16),
            pltpu.VMEM((ROWS, COLS), F32),
            pltpu.VMEM((CHUNKS, SPANS), jnp.int32),
            pltpu.VMEM((SPANS, CHUNKS, KMAX), jnp.int32),
            pltpu.VMEM((2, 2 * SPAN, 2 * SPAN), F32),
            pltpu.VMEM((2, SPAN, 3 * SPAN), BF16),
            pltpu.VMEM((2, 6 * SPAN, 2 * SPAN), BF16),
            pltpu.VMEM((GRID, 128), F32),
            pltpu.VMEM((NY - 1, GRID, 128), F32),
            pltpu.VMEM((2, 128, WIDTH), BF16),
            pltpu.VMEM((CHUNKS - ROW0, KMAX, COLS), F32),
            pltpu.VMEM((NY, LISTED, 128), F32),
            pltpu.VMEM((2, STEPS, HALF_LISTED, 128), F32),
            pltpu.VMEM((CHUNKS, NY, SPAN, COLS), F32),
            pltpu.VMEM((CHUNKS, NY, SPAN, COLS), F32),
            pltpu.VMEM((2, CHUNKS, 2, HALF, COLS), F32),
            pltpu.VMEM((2, CHUNKS, STEPS, HALF, COLS), F32),
            pltpu.VMEM((ROWS, COLS), F32),
            pltpu.VMEM((ROWS, COLS), F32),
            pltpu.VMEM((CHUNKS, NZ, PIECE, COLS), F32),
            pltpu.VMEM((CHUNKS, NZ - 1, PIECE, COLS), F32),
            pltpu.VMEM((CHUNKS, NX, PIECE, COLS), F32),
            pltpu.VMEM((CHUNKS, PIECE, COLS), F32),
            dma((CHUNKS + 4,)),
            dma,
            dma,
            dma,
            dma((CHUNKS, NY)),
            dma((2,)),
            dma((2, len(UNITS), STEPS)),
            dma,
            dma,
            dma((2,)),
            dma((2, STEPS)),
            dma,
            dma((len(UNITS),)),
            dma,
            dma((len(UNITS),)),
            dma,
            dma((len(UNITS),)),
        ],
        compiler_params=pltpu.CompilerParams(
            collective_id=0, has_side_effects=True, vmem_limit_bytes=VMEM_LIMIT
        ),
        cost_estimate=pl.CostEstimate(
            flops=10**9, bytes_accessed=5 * 10**6, transcendentals=0
        ),
    )(grad_parts, momentum, keep_counts, keep_blocks.transpose(0, 2, 1, 3), jnp.asarray(dct_tables()))
    return pl.pallas_call(
        put_out,
        out_shape=(
            jax.ShapeDtypeStruct((ROWS, COLS), F32),
            jax.ShapeDtypeStruct((1, ROWS, COLS), F32),
        ),
        in_specs=[anywhere] * 2,
        out_specs=(anywhere, anywhere),
        scratch_shapes=[dma((2,))],
    )(update.reshape(ROWS, COLS), residual)


def solution(mesh):
    return jax.shard_map(
        shards,
        mesh=mesh,
        in_specs=(
            P("rep", "fsdp", None, None),
            P("rep", None, "fsdp"),
            P("rep", None, "fsdp"),
            P("rep", None, "fsdp", None),
        ),
        out_specs=(P(None, "fsdp"), P("rep", None, "fsdp")),
        check_vma=False,
    )
```

```python
import functools

import jax
import jax.numpy as jnp
import numpy as np
from jax import lax
from jax.experimental import pallas as pl
from jax.experimental.pallas import tpu as pltpu
from jax.sharding import PartitionSpec as P

MESH = pl.DeviceIdType.MESH
F32 = jnp.float32
BF16 = jnp.bfloat16

SPAN = 64
GRID = 8
KMAX = 16
NZ, NX, NY, NCORE = 8, 4, 8, 2
ROWS, COLS, WIDE = 256, 384, 6144
CHUNKS = ROWS // SPAN
SPANS = COLS // SPAN
HALF = SPAN // 2
PIECE = SPAN // NZ
STEPS = NY - 1
VMEM_LIMIT = 62 * 2**20
DISTANCES = (4, 3, -3, 2, -2, 1, -1, 0)
SLOT = {d: i for i, d in enumerate(DISTANCES)}
HIGHEST = lax.Precision.HIGHEST
VMEM_LIMIT = 62 * 2**20
UNITS = ((0, 0, 3), (1, 0, 2), (1, 2, 3), (2, 0, 3), (3, 0, 3))
GROUPS = ((2, 0), (2, 1), (2, 2), (3, 0), (3, 1), (3, 2))
NG = len(GROUPS)
SKIP = 2 * GROUPS[0][1]
WIDTH = NG * 128
LISTED = 2 * NG * GRID
HALF_LISTED = LISTED // 2
ROW0 = GROUPS[0][0]
LATE = tuple(u for u in range(len(UNITS)) if UNITS[u][0] >= ROW0)
EXCHANGE, RING, SPREAD, PLACE, PICK, LIST, MASK, FINISH, OVER_X, GATHER, DECODE, LAST = range(12)
PROGRAM = (
    [(RING, 0, 0), (EXCHANGE, 0, 3, 8), (RING, 0, 1), (EXCHANGE, 1, 0, 8), (RING, 1, 0), (RING, 1, 1)]
    + [(RING, 2, 0), (RING, 2, 1), (EXCHANGE, 3, 0, 8), (EXCHANGE, 2, 0, 8), (SPREAD,), (RING, 0, 2)]
    + [(PICK, 4), (RING, 0, 3), (LIST, 0), (PICK, 3), (PICK, -3), (LIST, 1), (LIST, 2), (RING, 0, 4)]
    + [(RING, 0, 5), (RING, 1, 2), (PICK, 2), (PICK, -2), (LIST, 3), (LIST, 4), (RING, 0, 6)]
    + [(RING, 1, 3), (RING, 2, 2), (PICK, 1), (PICK, -1), (LIST, 5), (LIST, 6), (RING, 2, 3)]
    + [(MASK, 0), (RING, 1, 4), (FINISH, 0), (RING, 1, 5), (RING, 2, 4), (RING, 3, 0), (PICK, 0), (PLACE,)]
    + [(DECODE,), (RING, 4, 0), (RING, 1, 6), (RING, 2, 5), (RING, 2, 6), (RING, 3, 1), (RING, 4, 1)]
    + [(MASK, 1), (RING, 3, 2), (RING, 4, 2), (FINISH, 1), (FINISH, 2), (OVER_X, 0), (RING, 3, 3)]
    + [(RING, 4, 3), (OVER_X, 3), (RING, 3, 4), (RING, 4, 4), (OVER_X, 4), (GATHER, 0), (RING, 3, 5)]
    + [(RING, 4, 5), (GATHER, 3), (OVER_X, 1), (OVER_X, 2), (RING, 3, 6), (RING, 4, 6)]
    + [(GATHER, 4), (GATHER, 1), (GATHER, 2), (LAST, 3), (LAST, 4)]
)


def dct_tables():
    k = np.arange(SPAN, dtype=np.float64)[:, None]
    n = np.arange(SPAN, dtype=np.float64)[None, :]
    basis = np.cos(np.pi * (2.0 * n + 1.0) * k / (2.0 * SPAN)) * np.sqrt(2.0 / SPAN)
    basis[0] *= np.sqrt(0.5)
    pair = np.kron(np.eye(2), basis)
    return np.stack([pair.T, pair]).astype(np.float32)


def split_table(table, axis):
    high = table.astype(BF16)
    low = (table - high.astype(F32)).astype(BF16)
    return jnp.concatenate([high, high, low], axis=axis)


def split(values, axis):
    high = values.astype(BF16)
    low = (values - high.astype(F32)).astype(BF16)
    return jnp.concatenate([high, low, high], axis=axis)


def step_distance(direction, step):
    distance = 4 - (step + 1) // 2
    half = (step + direction) % 2
    return (distance if direction == 0 else -distance), half


def kernel(
    grad, momentum, counts, blocks, tables,
    update, residual,
    g_v, m_v, cnt_v, blk_v, tab_v, left_v, right_v,
    tile, tiles, spread_v, place_v, packed, brought, stage, other, first, ring, mask, res, inv, zbuf, xbuf, upd,
    load_sem, res_sem, upd_sem, pair_send, pair_recv, ring_send, ring_recv,
    tile_send, tile_recv, list_send, list_recv, z_send, z_recv, x_send, x_recv, a_send, a_recv,
):
    rep, fsdp = lax.axis_index("rep"), lax.axis_index("fsdp")
    z, x = rep // NX, rep % NX
    y, core = fsdp // NCORE, fsdp % NCORE
    peer = {"fsdp": y * NCORE + 1 - core}

    def at_y(d):
        return {"fsdp": lax.rem(y + d, NY) * NCORE + core}

    neighbours = (at_y(1), at_y(NY - 1))

    def at_z(d):
        return {"rep": lax.rem(z + d, NZ) * NX + x}

    def at_x(d):
        return {"rep": z * NX + lax.rem(x + d, NX)}

    partners = (
        [at_z(d) for d in (4, 3, 5, 2, 6, 1, 7)]
        + [at_x(d) for d in (2, 1, 3)]
        + [at_y(d) for d in (4, 3, 5, 2, 6, 1, 7)]
        + [peer]
    )

    barrier = pltpu.get_barrier_semaphore()
    for partner in partners:
        pl.semaphore_signal(barrier, inc=1, device_id=partner, device_id_type=MESH)

    small = [
        (counts.at[0], cnt_v), (blocks.at[0], blk_v),
        (tables, tab_v), (momentum.at[0], m_v),
    ]
    loads = [
        pltpu.make_async_copy(
            grad.at[0, 0, pl.ds(k * SPAN, SPAN), :],
            g_v.at[pl.ds(k * SPAN, SPAN), :],
            load_sem.at[k],
        )
        for k in range(CHUNKS)
    ] + [
        pltpu.make_async_copy(src, dst, load_sem.at[CHUNKS + i])
        for i, (src, dst) in enumerate(small)
    ]
    for i in (0, CHUNKS + 1, 1, CHUNKS, CHUNKS + 2, CHUNKS + 3, 3, 2):
        loads[i].start()

    def columns(distance, which, first_lane=0, width=COLS):
        target = lax.rem(y + distance + NY, NY) * NCORE + which
        return pl.ds(pl.multiple_of(target * COLS + first_lane, 128), width)

    def lanes(unit):
        _, low, high = UNITS[unit]
        return pl.ds(low * 128, (high - low) * 128)

    def moved(src, dst, send_sem, recv_sem, device):
        return pltpu.make_async_remote_copy(
            src_ref=src, dst_ref=dst, send_sem=send_sem, recv_sem=recv_sem,
            device_id=device, device_id_type=MESH,
        )

    def pair_copy(k, i):
        return moved(stage.at[k, i], other.at[k, i], pair_send, pair_recv.at[k, i], peer)

    def fill_stage(k, i):
        stage[k, i] = g_v[pl.ds(k * SPAN, SPAN), columns(DISTANCES[i], 1 - core)].astype(F32)

    exchanged = set()

    def need(k, distance):
        if (k, distance) not in exchanged:
            exchanged.add((k, distance))
            pair_copy(k, SLOT[distance]).wait_recv()

    def own(unit, distance, half):
        k, low, high = UNITS[unit]
        need(k, distance)
        return (
            g_v[
                pl.ds(k * SPAN + half * HALF, HALF),
                columns(distance, core, low * 128, (high - low) * 128),
            ].astype(F32)
            + other[k, SLOT[distance], pl.ds(half * HALF, HALF), lanes(unit)]
        )

    def ring_copy(direction, unit, step):
        k, window = UNITS[unit][0], lanes(unit)
        return moved(
            first.at[direction, k, step, :, window]
            if step < 2
            else ring.at[direction, k, step - 2, :, window],
            ring.at[direction, k, step, :, window],
            ring_send.at[direction],
            ring_recv.at[direction, unit, step],
            neighbours[direction],
        )

    def ring_step(unit, step):
        k, window = UNITS[unit][0], lanes(unit)
        for direction in (0, 1):
            distance, half = step_distance(direction, step)
            if distance == -4:
                distance = 4
            if step < 2:
                first[direction, k, step, :, window] = own(unit, distance, half)
            else:
                ring_copy(direction, unit, step - 2).wait_recv()
                ring[direction, k, step - 2, :, window] += own(unit, distance, half)
            ring_copy(direction, unit, step).start()

    def places(k):
        spread = jnp.where(
            lax.broadcasted_iota(jnp.int32, (SPANS, COLS), 1) // SPAN
            == lax.broadcasted_iota(jnp.int32, (SPANS, COLS), 0),
            1.0, 0.0,
        ).astype(BF16)
        numbers = lax.dot_general(
            blk_v[:, k, :].astype(F32).astype(BF16), spread, (((0,), (0,)), ((), ())),
            preferred_element_type=F32,
        )
        live = jnp.dot(
            cnt_v[...].astype(F32).astype(BF16), spread, preferred_element_type=F32
        )[k : k + 1, :]
        slot = lax.broadcasted_iota(jnp.int32, (KMAX, COLS), 0).astype(F32)
        column = lax.broadcasted_iota(jnp.int32, (KMAX, COLS), 1)
        place = numbers - ((column % SPAN) // GRID).astype(F32)
        return jnp.where(slot + 0.5 < live, place, -100.0)

    def make_mask(k):
        place = places(k)
        for u in range(GRID):
            hit = jnp.where(place == float(u * GRID), 1.0, 0.0)
            row = jnp.max(hit, axis=0, keepdims=True)
            mask[pl.ds(k * SPAN + u * GRID, GRID), :] = jnp.broadcast_to(row, (GRID, COLS))

    def make_tile():
        span = lax.broadcasted_iota(jnp.int32, (SPANS, 128), 0)
        lane = lax.broadcasted_iota(jnp.int32, (SPANS, 128), 1)
        total = jnp.zeros((GRID, 128), F32)
        for k in range(ROW0, CHUNKS):
            listed = blk_v[:, k, :].astype(F32).astype(BF16)
            at = span + (k - ROW0) * SPANS - SKIP
            for h in range(2):
                chosen = jnp.where((lane == at + 64 * h) & (at >= 0), 1.0, 0.0).astype(BF16)
                moved_out = lax.dot_general(
                    listed, chosen, (((0,), (0,)), ((), ())), preferred_element_type=F32
                )
                total = total + moved_out[h * GRID : (h + 1) * GRID]
        tile[...] = total

    def make_spread():
        lane = lax.broadcasted_iota(jnp.int32, (128, WIDTH), 0)
        span = lax.broadcasted_iota(jnp.int32, (128, WIDTH), 1) // SPAN
        for h in range(2):
            spread_v[h] = jnp.where(lane == span + 64 * h, 1.0, 0.0).astype(BF16)

    def tile_copy(d):
        return moved(tile, tiles.at[d - 1], tile_send, tile_recv, at_y(d))

    def listed_place(distance):
        source = tile[...] if distance == 0 else tiles[7 - distance % NY]
        column = lax.broadcasted_iota(jnp.int32, (GRID, WIDTH), 1)
        group = ((column % SPAN) // GRID).astype(F32)
        return jnp.concatenate(
            [
                jnp.dot(source.astype(BF16), spread_v[h], preferred_element_type=F32) - group
                for h in range(2)
            ],
            axis=0,
        )

    def lane_bit(size):
        lane = lax.broadcasted_iota(jnp.int32, (LISTED, 128), 1)
        return (lane // size) % 2 == 1

    def listed_sum(distance):
        fields = {}
        for k in range(ROW0, CHUNKS):
            rows = pl.ds(k * SPAN, SPAN)
            need(k, distance)
            field = g_v[rows, columns(distance, core)].astype(F32) + other[k, SLOT[distance]]
            if distance == 0:
                field = field + 0.9 * m_v[rows, :]
            fields[k] = field
        field = jnp.concatenate([fields[k][:, g * 128 : (g + 1) * 128] for k, g in GROUPS], axis=1)
        coeff = transform(field, 0)
        place = listed_place(distance)
        picked = []
        for slot in range(KMAX):
            where = jnp.broadcast_to(place[slot : slot + 1, :], (GRID, WIDTH))
            got = jnp.zeros((GRID, WIDTH), F32)
            for u in range(GRID):
                got = jnp.where(where == float(u * GRID), coeff[u * GRID : (u + 1) * GRID], got)
            picked.append(got)
        values = [
            jnp.concatenate(
                [
                    picked[h * GRID + j][:, g * 128 : (g + 1) * 128]
                    for h in range(2)
                    for g in range(NG)
                ],
                axis=0,
            )
            for j in range(GRID)
        ]
        for size in (32, 16, 8):
            bit = lane_bit(size)
            half = len(values) // 2
            merged = []
            for j in range(half):
                low, high = values[j], values[j + half]
                out = jnp.where(bit, low, high)
                out = jnp.where(bit, pltpu.roll(out, size, 1), pltpu.roll(out, 128 - size, 1))
                merged.append(jnp.where(bit, high, low) + out)
            values = merged
        packed[SLOT[distance]] = values[0]

    def half_rows(half):
        return pl.ds(half * HALF_LISTED, HALF_LISTED)

    def list_copy(direction, step):
        if step < 3:
            distance, half = step_distance(direction, step)
            source = packed.at[SLOT[4 if distance == -4 else distance], half_rows(half)]
        else:
            source = brought.at[direction, step - 2]
        return moved(
            source, brought.at[direction, step],
            list_send.at[direction], list_recv.at[direction, step],
            at_y((2, NY - 2)[direction]) if step == 0 else neighbours[direction],
        )

    def list_step(step):
        for direction in (0, 1):
            distance, half = step_distance(direction, step)
            if step >= 3:
                list_copy(direction, step - 2).wait_recv()
                more = packed[SLOT[distance], half_rows(half)]
                if step == 4:
                    list_copy(direction, 0).wait_recv()
                    more = more + brought[direction, 0]
                brought[direction, step - 2] += more
            list_copy(direction, step).start()

    def decode():
        for step in (STEPS - 2, STEPS - 1):
            for direction in (0, 1):
                list_copy(direction, step).wait_recv()
        own_part = packed[SLOT[0]]
        values = [
            own_part
            + jnp.concatenate(
                [
                    brought[0, STEPS - 1] + brought[1, STEPS - 2],
                    brought[0, STEPS - 2] + brought[1, STEPS - 1],
                ],
                axis=0,
            )
        ]
        for size in (8, 16, 32):
            bit = lane_bit(size)
            low, high = [], []
            for value in values:
                low.append(jnp.where(bit, pltpu.roll(value, size, 1), value))
                high.append(jnp.where(bit, value, pltpu.roll(value, 128 - size, 1)))
            values = low + high
        place = jnp.concatenate(
            [place_v[k - ROW0][:, g * 128 : (g + 1) * 128] for k, g in GROUPS], axis=1
        )
        kept = [jnp.zeros((GRID, WIDTH), F32)] * GRID
        for slot in range(KMAX):
            h, j = slot // GRID, slot % GRID
            at = [(h * NG + g) * GRID for g in range(NG)]
            value = jnp.concatenate([values[j][r : r + GRID] for r in at], axis=1)
            where = jnp.broadcast_to(place[slot : slot + 1, :], (GRID, WIDTH))
            kept = [
                jnp.where(where == float(u * GRID), value, kept[u]) for u in range(GRID)
            ]
        decoded = transform(jnp.concatenate(kept, axis=0), 1)
        for i, (k, g) in enumerate(GROUPS):
            window = pl.ds(g * 128, 128)
            inv[k, :, :, window] = decoded[:, i * 128 : (i + 1) * 128].reshape(NZ, PIECE, 128)
        for unit in LATE:
            for d in (4, 3, 5, 2, 6, 1, 7):
                z_copy(unit, d).start()

    def transform(values, way):
        groups = values.shape[1] // 128
        rows = jnp.dot(left_v[way], split(values, 0), preferred_element_type=F32)
        parts = jnp.concatenate([rows[:, g * 128 : (g + 1) * 128] for g in range(groups)], axis=0)
        done = jnp.dot(split(parts, 1), right_v[way], preferred_element_type=F32)
        return jnp.concatenate([done[g * SPAN : (g + 1) * SPAN] for g in range(groups)], axis=1)

    def z_copy(unit, d):
        k, window = UNITS[unit][0], lanes(unit)
        return moved(
            inv.at[k, lax.rem(z + d, NZ), :, window], zbuf.at[k, d - 1, :, window],
            z_send, z_recv.at[unit], at_z(d),
        )

    def x_copy(unit, d):
        k, window = UNITS[unit][0], lanes(unit)
        return moved(
            xbuf.at[k, x, :, window], xbuf.at[k, x, :, window],
            x_send, x_recv.at[unit], at_x(d),
        )

    def a_copy(unit, d):
        k, window = UNITS[unit][0], lanes(unit)
        return moved(
            upd.at[k, :, window], update.at[k, z, :, window],
            a_send, a_recv.at[unit], at_z(d),
        )

    def arrived(ref, sem):
        moved(ref, ref, z_send, sem, peer).wait_recv()

    def sent(ref, sem):
        moved(ref, ref, sem, z_recv.at[0], peer).wait_send()

    def residual_copy(unit):
        rows, window = pl.ds(UNITS[unit][0] * SPAN, SPAN), lanes(unit)
        return pltpu.make_async_copy(res.at[rows, window], residual.at[0, rows, window], res_sem)

    def update_copy(unit):
        k, window = UNITS[unit][0], lanes(unit)
        return pltpu.make_async_copy(upd.at[k, :, window], update.at[k, z, :, window], upd_sem)

    def summed(unit):
        k, window = UNITS[unit][0], lanes(unit)
        for step in (STEPS - 2, STEPS - 1):
            for direction in (0, 1):
                ring_copy(direction, unit, step).wait_recv()
        lower = (
            own(unit, 0, 0) + ring[0, k, STEPS - 1, :, window] + ring[1, k, STEPS - 2, :, window]
        )
        upper = (
            own(unit, 0, 1) + ring[0, k, STEPS - 2, :, window] + ring[1, k, STEPS - 1, :, window]
        )
        rows = pl.ds(k * SPAN, SPAN)
        return 0.9 * m_v[rows, window] + jnp.concatenate([lower, upper], axis=0)

    def finish(unit):
        k, window = UNITS[unit][0], lanes(unit)
        rows = pl.ds(k * SPAN, SPAN)
        fresh = summed(unit)
        decoded = transform(transform(fresh, 0) * mask[rows, window], 1)
        inv[k, :, :, window] = decoded.reshape(NZ, PIECE, decoded.shape[1])
        for d in (4, 3, 5, 2, 6, 1, 7):
            z_copy(unit, d).start()
        res[rows, window] = fresh - decoded
        residual_copy(unit).start()

    def last(unit):
        k, window = UNITS[unit][0], lanes(unit)
        rows = pl.ds(k * SPAN, SPAN)
        res[rows, window] = summed(unit) - inv[k, :, :, window].reshape(SPAN, COLS)
        residual_copy(unit).start()

    def over_x(unit):
        k, window = UNITS[unit][0], lanes(unit)
        arrived(zbuf.at[k, :, :, window], z_recv.at[unit])
        xbuf[k, x, :, window] = inv[k, z, :, window] + jnp.sum(zbuf[k, :, :, window], axis=0)
        for d in (2, 1, 3):
            x_copy(unit, d).start()

    def gather(unit):
        k, window = UNITS[unit][0], lanes(unit)
        arrived(xbuf.at[k, pl.ds(0, NX - 1), :, window], x_recv.at[unit])
        total = (xbuf[k, 0, :, window] + xbuf[k, 1, :, window]) + (
            xbuf[k, 2, :, window] + xbuf[k, 3, :, window]
        )
        upd[k, :, window] = total * (1.0 / (NZ * NX))
        for d in (4, 3, 5, 2, 6, 1, 7):
            a_copy(unit, d).start()
        update_copy(unit).start()

    def exchange(k, begin, end):
        if k > 0:
            loads[k].wait()
            for i in range(begin, end):
                fill_stage(k, i)
        for i in range(begin, end):
            pair_copy(k, i).start()

    def spread_tables():
        for i in (CHUNKS, CHUNKS + 2, CHUNKS + 3):
            loads[i].wait()
        for way in range(2):
            left_v[way] = split_table(tab_v[1 - way, :SPAN, :SPAN], 1)
            right_v[way] = split_table(tab_v[way], 0)
        make_spread()
        arrived(tiles, tile_recv)

    def late_places():
        for k in range(ROW0, CHUNKS):
            place_v[k - ROW0] = places(k)

    loads[0].wait()
    for i in range(NY):
        fill_stage(0, i)
    loads[CHUNKS + 1].wait()
    make_tile()
    pl.semaphore_wait(barrier, len(partners))
    exchange(0, 0, 3)
    for d in (4, 3, 5, 2, 6, 1, 7):
        tile_copy(d).start()

    tasks = {
        EXCHANGE: exchange, RING: ring_step, SPREAD: spread_tables, PLACE: late_places,
        PICK: listed_sum, LIST: list_step,
        MASK: make_mask, FINISH: finish, OVER_X: over_x, GATHER: gather, DECODE: decode, LAST: last,
    }
    for task, *what in PROGRAM:
        tasks[task](*what)

    pltpu.make_async_copy(res, residual.at[0], res_sem).wait()
    pltpu.make_async_copy(upd, update.at[:, z], upd_sem).wait()
    sent(stage, pair_send)
    sent(tiles, tile_send)
    for direction in (0, 1):
        sent(ring.at[direction], ring_send.at[direction])
        sent(brought.at[direction], list_send.at[direction])
    sent(zbuf, z_send)
    sent(xbuf.at[:, pl.ds(0, NX - 1)], x_send)
    for unit in range(len(UNITS)):
        arrived(zbuf.at[UNITS[unit][0], :, :, lanes(unit)], a_recv.at[unit])
    sent(zbuf, a_send)


def shards(grad_parts, momentum, keep_counts, keep_blocks):
    anywhere = pl.BlockSpec(memory_space=pl.ANY)
    outside = pl.BlockSpec(memory_space=pltpu.HBM)
    dma = pltpu.SemaphoreType.DMA
    update, residual = pl.pallas_call(
        kernel,
        out_shape=(
            pltpu.VMEM((CHUNKS, NZ, PIECE, COLS), F32),
            pltpu.VMEM((1, ROWS, COLS), F32),
        ),
        in_specs=[outside] * 5,
        out_specs=(anywhere, anywhere),
        scratch_shapes=[
            pltpu.VMEM((ROWS, WIDE), BF16),
            pltpu.VMEM((ROWS, COLS), F32),
            pltpu.VMEM((CHUNKS, SPANS), jnp.int32),
            pltpu.VMEM((SPANS, CHUNKS, KMAX), jnp.int32),
            pltpu.VMEM((2, 2 * SPAN, 2 * SPAN), F32),
            pltpu.VMEM((2, SPAN, 3 * SPAN), BF16),
            pltpu.VMEM((2, 6 * SPAN, 2 * SPAN), BF16),
            pltpu.VMEM((GRID, 128), F32),
            pltpu.VMEM((NY - 1, GRID, 128), F32),
            pltpu.VMEM((2, 128, WIDTH), BF16),
            pltpu.VMEM((CHUNKS - ROW0, KMAX, COLS), F32),
            pltpu.VMEM((NY, LISTED, 128), F32),
            pltpu.VMEM((2, STEPS, HALF_LISTED, 128), F32),
            pltpu.VMEM((CHUNKS, NY, SPAN, COLS), F32),
            pltpu.VMEM((CHUNKS, NY, SPAN, COLS), F32),
            pltpu.VMEM((2, CHUNKS, 2, HALF, COLS), F32),
            pltpu.VMEM((2, CHUNKS, STEPS, HALF, COLS), F32),
            pltpu.VMEM((ROWS, COLS), F32),
            pltpu.VMEM((ROWS, COLS), F32),
            pltpu.VMEM((CHUNKS, NZ, PIECE, COLS), F32),
            pltpu.VMEM((CHUNKS, NZ - 1, PIECE, COLS), F32),
            pltpu.VMEM((CHUNKS, NX, PIECE, COLS), F32),
            pltpu.VMEM((CHUNKS, PIECE, COLS), F32),
            dma((CHUNKS + 4,)),
            dma,
            dma,
            dma,
            dma((CHUNKS, NY)),
            dma((2,)),
            dma((2, len(UNITS), STEPS)),
            dma,
            dma,
            dma((2,)),
            dma((2, STEPS)),
            dma,
            dma((len(UNITS),)),
            dma,
            dma((len(UNITS),)),
            dma,
            dma((len(UNITS),)),
        ],
        compiler_params=pltpu.CompilerParams(
            collective_id=0, has_side_effects=True, vmem_limit_bytes=VMEM_LIMIT
        ),
        cost_estimate=pl.CostEstimate(
            flops=10**9, bytes_accessed=5 * 10**6, transcendentals=0
        ),
    )(grad_parts, momentum, keep_counts, keep_blocks.transpose(0, 2, 1, 3), jnp.asarray(dct_tables()))
    return update.reshape(ROWS, COLS), residual


def solution(mesh):
    return jax.shard_map(
        shards,
        mesh=mesh,
        in_specs=(
            P("rep", "fsdp", None, None),
            P("rep", None, "fsdp"),
            P("rep", None, "fsdp"),
            P("rep", None, "fsdp", None),
        ),
        out_specs=(P(None, "fsdp"), P("rep", None, "fsdp")),
        check_vma=False,
    )
```
